512 devices in a mesh: ctx: 128 (over y_lo, z, x), ch: 4 (over y_hi, core).
Axes of the slice: x: 4, y: 4 (y_hi: 2, y_lo: 2; y = y_hi * 2 + y_lo), z: 16, core: 2. Of those that a mesh axis runs over, the one named last changes fastest.
Arguments:
- q_branch: bfloat16 [4096, 16384], P('ch', 'ctx'), may hold values from -6 to 6
- k_branch: bfloat16 [4096, 16384], P('ch', 'ctx'), may hold values from -6 to 6
- v_branch: bfloat16 [4096, 16384], P('ch', 'ctx'), may hold values from -6 to 6
- grad_gated: bfloat16 [4096, 16384], P('ch', 'ctx'), may hold values from -6 to 6
- decay_rates: float32 [256, 16], replicated, as said below
- residue: float32 [256, 16], replicated, may hold values from -1.5 to 1.5
Outputs:
- grad_q: bfloat16 [4096, 16384], P('ch', 'ctx')
- grad_k: bfloat16 [4096, 16384], P('ch', 'ctx')
- grad_v: bfloat16 [4096, 16384], P('ch', 'ctx')
- grad_residue: float32 [256, 16], replicated
The draws below stay inside these ranges and needn't reach their ends.
Inputs may be any that keep to these rules, and one draw needn't show every extreme that they name: `decay_rates`: every rate lies between 0.05 / 16384 and 1 / 30.
All inputs are finite; a program needn't handle non-finite values.
Results may differ from the reference program's by a relative error of at most 0.0029.
Values sent between devices are 32-bit elements; how exact they have to be, the bound alone decides.
A program may use at most 128 MiB of HBM per device.

```python
import math
import jax
import jax.numpy as jnp
from jax import lax

CH = 4096
FGROUPS = 256
MODES = 16
TOKENS = 16384


def draw_decay_rates(key, part):
    key = jax.random.fold_in(key, 1)
    pick_key, slow_key, wide_key = jax.random.split(key, 3)
    share = 0.4
    pick = jax.random.uniform(pick_key, (FGROUPS, MODES), jnp.float32)
    slow = jnp.exp(jax.random.uniform(slow_key, (FGROUPS, MODES), jnp.float32, math.log(0.05), math.log(2.0))) / TOKENS
    wide = jnp.exp(jax.random.uniform(wide_key, (FGROUPS, MODES), jnp.float32, math.log(0.05 / TOKENS), math.log(1.0 / 30.0)))
    return jnp.where(pick < share, slow, wide).astype(jnp.float32)


def level_of(stream_key, extent, shards, smallest, top_value):
    def one(dim, blocks):
        steps = jax.random.uniform(jax.random.fold_in(jax.random.fold_in(stream_key, 6), dim), (blocks,), jnp.float32, smallest / len(shards), top_value / len(shards))
        return jnp.repeat(jnp.exp(steps), extent[dim] // blocks).reshape((-1,) + (1,) * (len(extent) - dim - 1))

    factor_of = one(*shards[0])
    for cut in shards[1:]:
        factor_of = factor_of * one(*cut)
    return factor_of


def centred(key, extent, scale, reach, shards=(), kind=jnp.bfloat16):
    drawn = jax.random.normal(key, extent, jnp.float32) * scale
    if len(shards) > 0:
        drawn = level_of(key, extent, shards, -0.22, 0.18) * drawn
    return jnp.clip(drawn, min=-reach, max=reach).astype(kind)


def setup_inputs(seed: int = 0) -> dict:
    arg_keys = jax.random.split(jax.random.key(seed), 7)
    return {
        "q_branch": centred(arg_keys[0], (CH, TOKENS), 1.0, 6.0, ((0, 4), (1, 128))),
        "k_branch": centred(arg_keys[1], (CH, TOKENS), 1.0, 6.0, ((0, 4), (1, 128))),
        "v_branch": centred(arg_keys[2], (CH, TOKENS), 1.0, 6.0, ((0, 4), (1, 128))),
        "grad_gated": centred(arg_keys[3], (CH, TOKENS), 1.0, 6.0, ((0, 4), (1, 128))),
        "decay_rates": draw_decay_rates(jax.random.fold_in(arg_keys[6], 71), 0),
        "residue": centred(arg_keys[5], (FGROUPS, MODES), MODES ** -0.5, 1.5, (), jnp.float32),
    }


def causal_conv(signal, kernel):
    length = signal.shape[1]
    padded = 2 * length
    spectrum = jnp.fft.rfft(signal, n=padded, axis=1) * jnp.fft.rfft(kernel, n=padded, axis=1)
    return jnp.fft.irfft(spectrum, n=padded, axis=1)[:, :length]

def reference(q_branch, k_branch, v_branch, grad_gated, decay_rates, residue):
    length = q_branch.shape[1]
    channels = q_branch.shape[0]
    repeats = channels // FGROUPS
    norm_factor = 1.0 / math.sqrt(length)
    rates = jnp.tile(decay_rates, (repeats, 1))
    scaled = jnp.tile(residue, (repeats, 1)) * jnp.sqrt(2.0 * rates)
    query_float = q_branch.astype(jnp.float32)
    key_float = k_branch.astype(jnp.float32)
    value_float = v_branch.astype(jnp.float32)
    product_kv = key_float * value_float
    positions = jnp.arange(length).astype(jnp.float32)
    filt = jnp.zeros(q_branch.shape, jnp.float32)
    for mode_index in range(MODES):
        filt = filt + scaled[:, mode_index, None] * jnp.exp(-rates[:, mode_index, None] * positions[None, :])
    conv_out = causal_conv(product_kv, filt)
    cotangent = grad_gated.astype(jnp.float32)
    grad_q = (cotangent * conv_out).astype(jnp.bfloat16)
    gated_grad = cotangent * query_float
    conv_grad = jnp.flip(causal_conv(jnp.flip(gated_grad, axis=1), filt), axis=1)
    grad_k = (conv_grad * value_float).astype(jnp.bfloat16)
    grad_v = (conv_grad * key_float).astype(jnp.bfloat16)
    columns = []
    for mode_index in range(MODES):
        kernel = jnp.exp(-rates[:, mode_index, None] * positions[None, :])
        state = causal_conv(product_kv, kernel)
        columns.append(jnp.sqrt(2.0 * rates[:, mode_index]) * lax.optimization_barrier(jnp.sum(gated_grad * state, axis=1)) * norm_factor)
    per_channel = jnp.stack(columns, axis=1)
    grad_residue = lax.optimization_barrier(jnp.sum(per_channel.reshape(repeats, FGROUPS, MODES), axis=0))
    return (grad_q, grad_k, grad_v, grad_residue)
```

```python
import functools
import math

import jax
import jax.numpy as jnp
from jax import lax
from jax.experimental import pallas as pl
from jax.experimental.pallas import tpu as pltpu
from jax.sharding import PartitionSpec as P

MESH = pl.DeviceIdType.MESH
F32 = jnp.float32

NX, NZ, NY, NCH = 4, 16, 2, 4
PLANE = NX * NY
MODES = 16
FG = 256
CHN = 1024
ROWS = 128
SUB = 8
GROUP = 8
BACK = (-4, 3, -3, 2, -2, 1, -1)
ACROSS = (8, 7, 9, 6, 10, 5, 11, 4, 12, 3, 13, 2, 14, 1, 15)
IN_PLANE = (6, 2, 5, 7, 3, 1, 4)


def tree_sum(terms):
    terms = list(terms)
    while len(terms) > 1:
        terms = [
            terms[i] + terms[i + 1] if i + 1 < len(terms) else terms[i]
            for i in range(0, len(terms), 2)
        ]
    return terms[0]


def scan_kernel(
    norm,
    q_hbm, k_hbm, v_hbm, g_hbm, rate_hbm, resid_hbm,
    gq_out, gk_out, gv_out, res_out,
    q_in, k_in, v_in, g_in, rate_in, resid_in,
    x_kv, x_g, c_out, c_grad,
    d_tab, w_tab, plane_decay_tab, block_decay_tab,
    a_send, a_recv, tot, b_send, b_recv, owner_out, c_recv, grp, e_send, e_recv,
    ch_recv, f_send, f_recv, in_sem, send_sem, recv_sem,
):
    ctx, ch = lax.axis_index("ctx"), lax.axis_index("ch")
    x, z, y = ctx % NX, (ctx // NX) % NZ, ctx // (NX * NZ)
    a = y * NX + x

    def plane_id(p):
        return ((p // NX) * NZ + z) * NX + p % NX, ch

    def z_id(zz):
        return (y * NZ + zz) * NX + x, ch

    plane = [(a + k) % PLANE for k in IN_PLANE]
    across = [(z + k) % NZ for k in ACROSS]
    others = [(ch + k) % NCH for k in range(1, NCH)]

    loads = [
        pltpu.make_async_copy(src, dst, in_sem.at[i])
        for i, (src, dst) in enumerate(
            [
                (k_hbm, k_in), (v_hbm, v_in), (g_hbm, g_in), (q_hbm, q_in),
                (rate_hbm, rate_in), (resid_hbm, resid_in),
            ]
        )
    ]
    for load in loads:
        load.start()

    barrier = pltpu.get_barrier_semaphore()
    for zz in across:
        pl.semaphore_signal(barrier, inc=1, device_id=z_id(zz), device_id_type=MESH)
    for p in plane:
        pl.semaphore_signal(barrier, inc=1, device_id=plane_id(p), device_id_type=MESH)
    for c in others:
        pl.semaphore_signal(barrier, inc=1, device_id=(ctx, c), device_id_type=MESH)

    loads[4].wait()
    loads[5].wait()
    rate_t = rate_in[...]
    weight_t = resid_in[...] * jnp.sqrt(2.0 * rate_t)
    odd = lax.broadcasted_iota(jnp.int32, (SUB, ROWS), 0) % 2 == 1
    for m in range(MODES):
        rate = jnp.where(odd, rate_t[m : m + 1, ROWS:], rate_t[m : m + 1, :ROWS])
        d_tab[m] = jnp.exp(-rate)
        block_decay_tab[m] = jnp.exp(-rate * ROWS)
        plane_decay_tab[m] = jnp.exp(-rate * (ROWS * NX))
        w_tab[m] = jnp.where(odd, weight_t[m : m + 1, ROWS:], weight_t[m : m + 1, :ROWS])

    loads[0].wait()
    loads[1].wait()
    for j in range(SUB):
        rows = pl.ds(j * ROWS, ROWS)
        product = k_in[rows, :].astype(F32) * v_in[rows, :].astype(F32)
        x_kv[pl.ds(j, ROWS, stride=SUB), :] = product.T
    loads[2].wait()
    loads[3].wait()
    for j in range(SUB):
        rows = pl.ds(j * ROWS, ROWS)
        product = g_in[rows, :].astype(F32) * q_in[rows, :].astype(F32)
        x_g[pl.ds(j, ROWS, stride=SUB), :] = product.T

    def at(t):
        return pl.ds(pl.multiple_of(t * SUB, SUB), SUB)

    zero = jnp.zeros((SUB, ROWS), F32)
    for first in range(0, MODES, GROUP):
        modes = range(first, first + GROUP)
        d = [d_tab[m] for m in modes]
        w = [w_tab[m] for m in modes]

        def local_step(t, carry, d=d, w=w, first=first):
            ahead, back, acc = carry
            here, there = at(t), at(ROWS - 1 - t)
            value, grad, late = x_kv[here, :], x_g[here, :], x_g[there, :]
            ahead = tuple(d[i] * ahead[i] + value for i in range(GROUP))
            back = tuple(d[i] * back[i] + late for i in range(GROUP))
            acc = tuple(acc[i] + grad * ahead[i] for i in range(GROUP))
            out = tree_sum(w[i] * ahead[i] for i in range(GROUP))
            out_grad = tree_sum(w[i] * back[i] for i in range(GROUP))
            if first:
                out = out + c_out[here, :]
                out_grad = out_grad + c_grad[there, :]
            c_out[here, :] = out
            c_grad[there, :] = out_grad
            return ahead, back, acc

        start = ((zero,) * GROUP,) * 3
        ahead, back, acc = lax.fori_loop(0, ROWS, local_step, start, unroll=4)
        for i, m in enumerate(modes):
            a_send[m // 2, m % 2] = ahead[i]
            a_send[m // 2, 2 + m % 2] = back[i]
            a_send[m // 2, 4 + m % 2] = acc[i]

    pl.semaphore_wait(barrier, len(plane) + len(across) + len(others))

    sent = []

    def send(src, dst, sem, device):
        copy = pltpu.make_async_remote_copy(
            src_ref=src, dst_ref=dst, send_sem=send_sem.at[sem], recv_sem=recv_sem.at[sem],
            device_id=device, device_id_type=MESH,
        )
        copy.start()
        sent.append(copy)
        return copy

    copies = [
        send(a_send.at[p], a_recv.at[a], i, plane_id(p)) for i, p in enumerate(plane)
    ]
    a_recv[a] = a_send[a]
    mine = pl.ds(2 * a, 2)
    d2, block_decay, plane_decay = d_tab[mine], block_decay_tab[mine], plane_decay_tab[mine]
    for copy in copies:
        copy.wait_recv()

    resid = jnp.zeros((2, SUB, ROWS), F32)
    for yy in range(NY):
        run = jnp.zeros((2, SUB, ROWS), F32)
        for xx in range(NX):
            slot = yy * NX + xx
            resid = resid + a_recv[slot, 4:6] + d2 * a_recv[slot, 2:4] * run
            run = block_decay * run + a_recv[slot, 0:2]
        tot[yy] = run
        run = jnp.zeros((2, SUB, ROWS), F32)
        for xx in reversed(range(NX)):
            run = block_decay * run + a_recv[yy * NX + xx, 2:4]
        tot[2 + yy] = run
    tot[4] = resid
    tot[5] = plane_decay
    tot[6] = d2

    for p in range(SUB):
        for item in range(5):
            b_send[p, item] = tot[item, p // 4, 2 * (p % 4) : 2 * (p % 4) + 2, :]
    base = len(plane)
    copies = [
        send(b_send.at[zz % SUB], b_recv.at[z], base + i, z_id(zz)) for i, zz in enumerate(across)
    ]
    b_recv[z] = b_send[z % SUB]
    pair = z % SUB
    decay_rows = tot_rows(tot, 5, pair)
    step_rows = tot_rows(tot, 6, pair)
    for copy in copies:
        copy.wait_recv()

    run = jnp.zeros((2, ROWS), F32)
    total = jnp.zeros((2, ROWS), F32)
    for yy in range(NY):
        for zz in range(NZ):
            owner_out[zz, yy] = run
            total = total + step_rows * b_recv[zz, 2 + yy] * run
            run = decay_rows * run + b_recv[zz, yy]
    run = jnp.zeros((2, ROWS), F32)
    for yy in reversed(range(NY)):
        for zz in reversed(range(NZ)):
            owner_out[zz, 2 + yy] = run
            run = decay_rows * run + b_recv[zz, 2 + yy]
    for zz in range(NZ):
        total = total + b_recv[zz, 4]
    for zz in range(NZ):
        owner_out[zz, 4] = total

    base += len(across)
    copies = [
        send(owner_out.at[(z + k) % NZ], c_recv.at[pair], base + i, z_id((z + k) % NZ))
        for i, k in enumerate(BACK)
    ]
    c_recv[pair] = owner_out[z]
    for copy in copies:
        copy.wait_recv()

    for i in range(2):
        ch_recv[ch, i] = (c_recv[4 * i, 4] + c_recv[4 * i + 1, 4]) + (
            c_recv[4 * i + 2, 4] + c_recv[4 * i + 3, 4]
        )
    base += len(BACK)
    ch_copies = [
        send(ch_recv.at[ch], ch_recv.at[ch], base + i, (ctx, c)) for i, c in enumerate(others)
    ]

    for p in range(SUB):
        for item in range(4):
            grp[item, p // 4, 2 * (p % 4) : 2 * (p % 4) + 2, :] = c_recv[p, item]
    for yy in range(NY):
        run = grp[yy]
        for xx in range(NX):
            slot = yy * NX + xx
            e_send[slot, 0:2] = run
            run = block_decay * run + a_recv[slot, 0:2]
        run = grp[2 + yy]
        for xx in reversed(range(NX)):
            slot = yy * NX + xx
            e_send[slot, 2:4] = run
            run = block_decay * run + a_recv[slot, 2:4]
    base += len(others)
    copies = [
        send(e_send.at[p], e_recv.at[a], base + i, plane_id(p)) for i, p in enumerate(plane)
    ]
    e_recv[a] = e_send[a]
    base += len(plane)

    for copy in ch_copies:
        copy.wait_recv()
    f_send[...] = (ch_recv[0] + ch_recv[1]) + (ch_recv[2] + ch_recv[3])
    f_copies = [send(f_send, f_recv.at[a], base + i, plane_id(p)) for i, p in enumerate(plane)]
    f_recv[a] = f_send[...]

    for copy in copies:
        copy.wait_recv()

    d = [d_tab[m] for m in range(MODES)]
    w = [w_tab[m] for m in range(MODES)]
    ahead = tuple(w[m] * e_recv[m // 2, m % 2] for m in range(MODES))
    back = tuple(w[m] * e_recv[m // 2, 2 + m % 2] for m in range(MODES))

    def carry_step(t, carry):
        ahead, back = carry
        here, there = at(t), at(ROWS - 1 - t)
        ahead = tuple(d[m] * ahead[m] for m in range(MODES))
        back = tuple(d[m] * back[m] for m in range(MODES))
        c_out[here, :] = c_out[here, :] + tree_sum(ahead)
        c_grad[there, :] = c_grad[there, :] + tree_sum(back)
        return ahead, back

    lax.fori_loop(0, ROWS, carry_step, (ahead, back), unroll=4)

    for j in range(SUB):
        rows = pl.ds(j * ROWS, ROWS)
        lanes = pl.ds(j, ROWS, stride=SUB)
        gq_out[rows, :] = (g_in[rows, :].astype(F32) * c_out[lanes, :].T).astype(jnp.bfloat16)
        conv_grad = c_grad[lanes, :].T
        gk_out[rows, :] = (conv_grad * v_in[rows, :].astype(F32)).astype(jnp.bfloat16)
        gv_out[rows, :] = (conv_grad * k_in[rows, :].astype(F32)).astype(jnp.bfloat16)

    for copy in f_copies:
        copy.wait_recv()
    for m in range(MODES):
        for odd_half in range(2):
            cols = pl.ds(odd_half * ROWS, ROWS)
            res_out[m : m + 1, cols] = f_recv[m // 2, m % 2, odd_half : odd_half + 1, :]
    res_out[...] = res_out[...] * (jnp.sqrt(2.0 * rate_in[...]) * norm)
    for copy in sent:
        copy.wait_send()


def tot_rows(tot, item, pair):
    rows = jnp.zeros((2, ROWS), F32)
    for p in range(SUB):
        piece = tot[item, p // 4, 2 * (p % 4) : 2 * (p % 4) + 2, :]
        rows = jnp.where(pair == p, piece, rows)
    return rows


def scan_call(norm, q, k, v, g, rates, residue):
    hbm = pl.BlockSpec(memory_space=pltpu.HBM)
    vmem = pl.BlockSpec(memory_space=pltpu.VMEM)
    big = pltpu.VMEM((CHN, ROWS), F32)
    half = pltpu.VMEM((CHN, ROWS), jnp.bfloat16)
    table = pltpu.VMEM((MODES, SUB, ROWS), F32)
    small = pltpu.VMEM((MODES, FG), F32)
    copies = 3 * (PLANE - 1) + NZ - 1 + len(BACK) + NCH - 1
    wide = jax.ShapeDtypeStruct((CHN, ROWS), jnp.bfloat16)
    return pl.pallas_call(
        functools.partial(scan_kernel, norm),
        out_shape=(wide, wide, wide, jax.ShapeDtypeStruct((MODES, FG), F32)),
        in_specs=[hbm] * 6,
        out_specs=(vmem,) * 4,
        scratch_shapes=[
            half, half, half, half, small, small,
            big, big, big, big,
            table, table, table, table,
            pltpu.VMEM((PLANE, 6, SUB, ROWS), F32),
            pltpu.VMEM((PLANE, 6, SUB, ROWS), F32),
            pltpu.VMEM((7, 2, SUB, ROWS), F32),
            pltpu.VMEM((SUB, 5, 2, ROWS), F32),
            pltpu.VMEM((NZ, 5, 2, ROWS), F32),
            pltpu.VMEM((NZ, 5, 2, ROWS), F32),
            pltpu.VMEM((SUB, 5, 2, ROWS), F32),
            pltpu.VMEM((4, 2, SUB, ROWS), F32),
            pltpu.VMEM((PLANE, 4, SUB, ROWS), F32),
            pltpu.VMEM((PLANE, 4, SUB, ROWS), F32),
            pltpu.VMEM((NCH, 2, 2, ROWS), F32),
            pltpu.VMEM((2, 2, ROWS), F32),
            pltpu.VMEM((PLANE, 2, 2, ROWS), F32),
            pltpu.SemaphoreType.DMA((6,)),
            pltpu.SemaphoreType.DMA((copies,)),
            pltpu.SemaphoreType.DMA((copies,)),
        ],
        compiler_params=pltpu.CompilerParams(
            collective_id=0, has_side_effects=True, vmem_limit_bytes=63 * 2**20
        ),
        name="scan_states",
    )(q, k, v, g, rates, residue)


def finish_kernel(*refs):
    half = (len(refs) - 2) // 3
    srcs, dsts, held = refs[:half], refs[half : 2 * half], refs[2 * half : 3 * half]
    in_sem, out_sem = refs[3 * half :]
    loads = [pltpu.make_async_copy(srcs[i], held[i], in_sem.at[i]) for i in range(half)]
    stores = [pltpu.make_async_copy(held[i], dsts[i], out_sem.at[i]) for i in range(half)]
    for load in loads:
        load.start()
    for load, store in zip(loads, stores):
        load.wait()
        store.start()
    for store in stores:
        store.wait()


def finish_call(*results):
    n = len(results)
    hbm = pl.BlockSpec(memory_space=pl.ANY)
    return pl.pallas_call(
        finish_kernel,
        out_shape=tuple(jax.ShapeDtypeStruct(r.shape, r.dtype) for r in results),
        in_specs=[hbm] * n,
        out_specs=(hbm,) * n,
        scratch_shapes=[pltpu.VMEM(r.shape, r.dtype) for r in results]
        + [pltpu.SemaphoreType.DMA((n,)), pltpu.SemaphoreType.DMA((n,))],
        name="finish",
    )(*results)


def local(q_branch, k_branch, v_branch, grad_gated, decay_rates, residue):
    norm = 1.0 / math.sqrt(q_branch.shape[1] * lax.axis_size("ctx"))
    grad_q, grad_k, grad_v, res = finish_call(
        *scan_call(norm, q_branch, k_branch, v_branch, grad_gated, decay_rates.T, residue.T)
    )
    return grad_q, grad_k, grad_v, res.T


def solution(mesh):
    in_specs = (P("ch", "ctx"), P("ch", "ctx"), P("ch", "ctx"), P("ch", "ctx"), P(), P())
    out_specs = (P("ch", "ctx"), P("ch", "ctx"), P("ch", "ctx"), P())
    return jax.shard_map(local, mesh=mesh, in_specs=in_specs, out_specs=out_specs, check_vma=False)
```

```python
import functools
import math

import jax
import jax.numpy as jnp
from jax import lax
from jax.experimental import pallas as pl
from jax.experimental.pallas import tpu as pltpu
from jax.sharding import PartitionSpec as P

MESH = pl.DeviceIdType.MESH
F32 = jnp.float32

NX, NZ, NY, NCH = 4, 16, 2, 4
PLANE = NX * NY
MODES = 16
FG = 256
CHN = 1024
ROWS = 128
SUB = 8
GROUP = 8
HOME = 0
ANSWER_FIRST = (1, 2, 3)
ANSWER_LATER = (4, 5, 6, 7, 15, 8, 14, 9, 13, 10, 12, 11)
NEAR = ((0, 1), (0, 3), (1, 0))
FAR = ((1, 2), (1, 1), (1, 3), (0, 2))


def tree_sum(terms):
    terms = list(terms)
    while len(terms) > 1:
        terms = [
            terms[i] + terms[i + 1] if i + 1 < len(terms) else terms[i]
            for i in range(0, len(terms), 2)
        ]
    return terms[0]


def scan_kernel(
    norm,
    q_hbm, k_hbm, v_hbm, g_hbm, rate_hbm, resid_hbm,
    gq_hbm, gk_hbm, gv_hbm, res_out,
    q_in, k_in, v_in, g_in, rate_in, resid_in,
    x_kv, x_g, c_out, c_grad, gq_out, gk_out, gv_out,
    d_tab, w_tab, plane_decay_tab, block_decay_tab,
    a_send, a_recv, rows_tmp, b_send, b_recv, owner_out, c_recv, r_send, r_recv, e_send, e_recv,
    f_send, f_recv, in_sem, out_sem,
    a_send_sem, a_recv_sem, b_send_sem, b_recv_sem, c_send_sem, c_recv_sem,
    r_send_sem, r_recv_sem, e_send_sem, e_recv_sem, f_send_sem, f_recv_sem,
):
    ctx, ch = lax.axis_index("ctx"), lax.axis_index("ch")
    y, z, x = lax.div(ctx, NX * NZ), lax.rem(lax.div(ctx, NX), NZ), lax.rem(ctx, NX)
    a = y * NX + x
    is_home = z == HOME
    x_plus = [lax.rem(x + k, NX) for k in range(NX)]
    y_plus = [lax.rem(y + k, NY) for k in range(NY)]
    ch_plus = [lax.rem(ch + k, NCH) for k in range(NCH)]
    column = y * (NZ * NX) + x

    plane = [y_plus[dy] * NX + x_plus[dx] for dy, dx in FAR + NEAR]
    plane_ids = [((y_plus[dy] * NZ + z) * NX + x_plus[dx], ch) for dy, dx in FAR + NEAR]

    def z_id(zz, dch=0):
        return column + zz * NX, ch_plus[dch]

    loads = [
        pltpu.make_async_copy(src, dst, in_sem.at[i])
        for i, (src, dst) in enumerate(
            [
                (k_hbm, k_in), (v_hbm, v_in), (g_hbm, g_in), (q_hbm, q_in),
                (rate_hbm, rate_in), (resid_hbm, resid_in),
            ]
        )
    ]
    for i in (4, 5, 0, 1, 2, 3):
        loads[i].start()

    barrier = pltpu.get_barrier_semaphore()

    def greet(device):
        pl.semaphore_signal(barrier, inc=1, device_id=device, device_id_type=MESH)

    for device in plane_ids:
        greet(device)

    @pl.when(jnp.logical_not(is_home))
    def _():
        for k in range(NCH):
            greet(z_id(HOME, k))

    @pl.when(is_home)
    def _():
        for k in range(1, NCH):
            greet(z_id(HOME, k))

        @pl.loop(0, NZ)
        def _(zz):
            @pl.when(zz != HOME)
            def _():
                for k in range(NCH):
                    greet(z_id(zz, k))

    loads[4].wait()
    loads[5].wait()
    rate_t = rate_in[...]
    weight_t = resid_in[...] * jnp.sqrt(2.0 * rate_t)
    odd = lax.broadcasted_iota(jnp.int32, (SUB, ROWS), 0) % 2 == 1
    for m in range(MODES):
        rate = jnp.where(odd, rate_t[m : m + 1, ROWS:], rate_t[m : m + 1, :ROWS])
        d_tab[m] = jnp.exp(-rate)
        block_decay_tab[m] = jnp.exp(-rate * ROWS)
        plane_decay_tab[m] = jnp.exp(-rate * (ROWS * NX))
        w_tab[m] = jnp.where(odd, weight_t[m : m + 1, ROWS:], weight_t[m : m + 1, :ROWS])

    loads[0].wait()
    loads[1].wait()
    for j in range(SUB):
        rows = pl.ds(j * ROWS, ROWS)
        product = k_in[rows, :].astype(F32) * v_in[rows, :].astype(F32)
        x_kv[pl.ds(j, ROWS, stride=SUB), :] = product.T
    loads[2].wait()
    loads[3].wait()
    for j in range(SUB):
        rows = pl.ds(j * ROWS, ROWS)
        product = g_in[rows, :].astype(F32) * q_in[rows, :].astype(F32)
        x_g[pl.ds(j, ROWS, stride=SUB), :] = product.T

    def at(t):
        return pl.ds(pl.multiple_of(t * SUB, SUB), SUB)

    zero = jnp.zeros((SUB, ROWS), F32)
    for p in range(PLANE):
        a_send[p, 4] = zero
    for first in range(0, MODES, GROUP):
        modes = range(first, first + GROUP)
        d = [d_tab[m] for m in modes]

        def end_step(t, carry, d=d):
            ahead, back, acc = carry
            here, there = at(t), at(ROWS - 1 - t)
            value, grad, late = x_kv[here, :], x_g[here, :], x_g[there, :]
            ahead = tuple(d[i] * ahead[i] + value for i in range(GROUP))
            back = tuple(d[i] * back[i] + late for i in range(GROUP))
            acc = tuple(acc[i] + grad * ahead[i] for i in range(GROUP))
            return ahead, back, acc

        start = ((zero,) * GROUP,) * 3
        ahead, back, acc = lax.fori_loop(0, ROWS, end_step, start, unroll=4)
        for i, m in enumerate(modes):
            a_send[m // 2, m % 2] = ahead[i]
            a_send[m // 2, 2 + m % 2] = back[i]
            rows = 2 * (m % 2)
            a_send[m // 2, 4, rows : rows + 2, :] = tree_sum(
                acc[i][2 * r : 2 * r + 2, :] for r in range(4)
            )

    pl.semaphore_wait(barrier, len(plane) + jnp.where(is_home, NZ * NCH - 1, NCH))

    def remote(src, dst, send_sem, recv_sem, device):
        return pltpu.make_async_remote_copy(
            src_ref=src, dst_ref=dst, send_sem=send_sem, recv_sem=recv_sem,
            device_id=device, device_id_type=MESH,
        )

    a_copies = [
        remote(a_send.at[p], a_recv.at[a], a_send_sem.at[i], a_recv_sem.at[i], device)
        for i, (p, device) in enumerate(zip(plane, plane_ids))
    ]
    for copy in a_copies:
        copy.start()
    a_recv[a] = a_send[a]

    for first in range(0, MODES, GROUP):
        modes = range(first, first + GROUP)
        d = [d_tab[m] for m in modes]
        w = [w_tab[m] for m in modes]

        def local_step(t, carry, d=d, w=w, first=first):
            ahead, back = carry
            here, there = at(t), at(ROWS - 1 - t)
            value, late = x_kv[here, :], x_g[there, :]
            ahead = tuple(d[i] * ahead[i] + value for i in range(GROUP))
            back = tuple(d[i] * back[i] + late for i in range(GROUP))
            out = tree_sum(w[i] * ahead[i] for i in range(GROUP))
            out_grad = tree_sum(w[i] * back[i] for i in range(GROUP))
            if first:
                out = out + c_out[here, :]
                out_grad = out_grad + c_grad[there, :]
            c_out[here, :] = out
            c_grad[there, :] = out_grad
            return ahead, back

        lax.fori_loop(0, ROWS, local_step, ((zero,) * GROUP,) * 2, unroll=4)

    mine = pl.ds(2 * a, 2)
    d2, block_decay, plane_decay = d_tab[mine], block_decay_tab[mine], plane_decay_tab[mine]
    for copy in a_copies:
        copy.wait_recv()

    def over_repeats(value):
        rows_tmp[...] = value
        return [tree_sum(rows_tmp[i, 2 * r : 2 * r + 2, :] for r in range(4)) for i in range(2)]

    cross = jnp.zeros((2, SUB, ROWS), F32)
    for yy in range(NY):
        run = jnp.zeros((2, SUB, ROWS), F32)
        for xx in range(NX):
            slot = yy * NX + xx
            cross = cross + d2 * a_recv[slot, 2:4] * run
            run = block_decay * run + a_recv[slot, 0:2]
        b_send[2 * yy : 2 * yy + 2] = run
        run = jnp.zeros((2, SUB, ROWS), F32)
        for xx in reversed(range(NX)):
            run = block_decay * run + a_recv[yy * NX + xx, 2:4]
        b_send[4 + 2 * yy : 6 + 2 * yy] = run
    b_send[8] = tree_sum(a_recv[slot, 4] for slot in range(PLANE))
    for i, rows in enumerate(over_repeats(cross)):
        b_send[8, 2 * i : 2 * i + 2, :] = b_send[8, 2 * i : 2 * i + 2, :] + rows

    def to_home(zz):
        return remote(b_send, b_recv.at[zz], b_send_sem, b_recv_sem.at[zz], z_id(HOME))

    def answer(zz):
        return remote(owner_out.at[zz], c_recv, c_send_sem.at[zz], c_recv_sem, z_id(zz))

    def result(zz, k):
        return remote(
            r_send, r_recv.at[ch], r_send_sem.at[zz * NCH + k], r_recv_sem.at[k], z_id(zz, k)
        )

    @pl.when(jnp.logical_not(is_home))
    def _():
        to_home(z).start()

    @pl.when(is_home)
    def _():
        b_recv[HOME] = b_send[...]
        for zz in range(NZ):
            if zz != HOME:
                to_home(zz).wait_recv()
        run = jnp.zeros((2, SUB, ROWS), F32)
        cross = jnp.zeros((2, SUB, ROWS), F32)
        for yy in range(NY):
            for zz in range(NZ):
                owner_out[zz, 2 * yy : 2 * yy + 2] = run
                cross = cross + d2 * b_recv[zz, 4 + 2 * yy : 6 + 2 * yy] * run
                run = plane_decay * run + b_recv[zz, 2 * yy : 2 * yy + 2]
        run = jnp.zeros((2, SUB, ROWS), F32)
        for yy in reversed(range(NY)):
            for zz in reversed(range(NZ)):
                owner_out[zz, 4 + 2 * yy : 6 + 2 * yy] = run
                run = plane_decay * run + b_recv[zz, 4 + 2 * yy : 6 + 2 * yy]
        for zz in ANSWER_FIRST:
            answer(zz).start()
        within = tree_sum(b_recv[zz, 8] for zz in range(NZ))
        for i, rows in enumerate(over_repeats(cross)):
            r_send[i] = rows + within[2 * i : 2 * i + 2, :]
        for k in range(1, NCH):
            result(HOME, k).start()
        r_recv[ch] = r_send[...]
        c_recv[...] = owner_out[HOME]

    @pl.when(jnp.logical_not(is_home))
    def _():
        answer(z).wait_recv()

    for yy in range(NY):
        run = c_recv[2 * yy : 2 * yy + 2]
        for xx in range(NX):
            slot = yy * NX + xx
            e_send[slot, 0:2] = run
            run = block_decay * run + a_recv[slot, 0:2]
        run = c_recv[4 + 2 * yy : 6 + 2 * yy]
        for xx in reversed(range(NX)):
            slot = yy * NX + xx
            e_send[slot, 2:4] = run
            run = block_decay * run + a_recv[slot, 2:4]
    e_copies = [
        remote(e_send.at[p], e_recv.at[a], e_send_sem.at[i], e_recv_sem.at[i], device)
        for i, (p, device) in enumerate(zip(plane, plane_ids))
    ]
    for copy in e_copies:
        copy.start()
    e_recv[a] = e_send[a]

    @pl.when(is_home)
    def _():
        for zz in ANSWER_FIRST:
            for k in range(NCH):
                result(zz, k).start()
        for zz in ANSWER_LATER:
            answer(zz).start()
            for k in range(NCH):
                result(zz, k).start()

    pl.when(jnp.logical_not(is_home))(result(z, 0).wait_recv)
    for k in range(1, NCH):
        result(z, k).wait_recv()
    f_send[...] = (r_recv[0] + r_recv[1]) + (r_recv[2] + r_recv[3])
    f_copies = [
        remote(f_send, f_recv.at[a], f_send_sem.at[i], f_recv_sem.at[i], device)
        for i, device in enumerate(plane_ids)
    ]
    for copy in f_copies:
        copy.start()
    f_recv[a] = f_send[...]

    for slots, copies in (
        ([a] + plane[len(FAR) :], e_copies[len(FAR) :]),
        (plane[: len(FAR)], e_copies[: len(FAR)]),
    ):
        for copy in copies:
            copy.wait_recv()
        pairs = [(slot, i) for slot in slots for i in range(2)]
        d = [d_tab[2 * slot + i] for slot, i in pairs]
        w = [w_tab[2 * slot + i] for slot, i in pairs]
        ahead = tuple(w[n] * e_recv[slot, i] for n, (slot, i) in enumerate(pairs))
        back = tuple(w[n] * e_recv[slot, 2 + i] for n, (slot, i) in enumerate(pairs))

        def carry_step(t, carry, d=d):
            ahead, back = carry
            here, there = at(t), at(ROWS - 1 - t)
            ahead = tuple(d[n] * ahead[n] for n in range(GROUP))
            back = tuple(d[n] * back[n] for n in range(GROUP))
            c_out[here, :] = c_out[here, :] + tree_sum(ahead)
            c_grad[there, :] = c_grad[there, :] + tree_sum(back)
            return ahead, back

        lax.fori_loop(0, ROWS, carry_step, (ahead, back), unroll=4)

    stores = []
    for j in range(SUB):
        rows = pl.ds(j * ROWS, ROWS)
        lanes = pl.ds(j, ROWS, stride=SUB)
        gq_out[rows, :] = (g_in[rows, :].astype(F32) * c_out[lanes, :].T).astype(jnp.bfloat16)
        conv_grad = c_grad[lanes, :].T
        gk_out[rows, :] = (conv_grad * v_in[rows, :].astype(F32)).astype(jnp.bfloat16)
        gv_out[rows, :] = (conv_grad * k_in[rows, :].astype(F32)).astype(jnp.bfloat16)
        if j % 2 == 1:
            rows = pl.ds((j - 1) * ROWS, 2 * ROWS)
            for src, dst in ((gq_out, gq_hbm), (gk_out, gk_hbm), (gv_out, gv_hbm)):
                store = pltpu.make_async_copy(
                    src.at[rows, :], dst.at[rows, :], out_sem.at[len(stores)]
                )
                store.start()
                stores.append(store)

    for copy in f_copies:
        copy.wait_recv()
    for m in range(MODES):
        for half in range(2):
            cols = slice(half * ROWS, (half + 1) * ROWS)
            res_out[m : m + 1, cols] = f_recv[m // 2, m % 2, half : half + 1, :]
    res_out[...] = res_out[...] * (jnp.sqrt(2.0 * rate_in[...]) * norm)

    for copy in a_copies + e_copies + f_copies:
        copy.wait_send()
    @pl.when(jnp.logical_not(is_home))
    def _():
        to_home(z).wait_send()

    @pl.when(is_home)
    def _():
        @pl.loop(0, NZ)
        def _(zz):
            pl.when(zz != HOME)(lambda: answer(zz).wait_send())
            pl.when(zz != HOME)(lambda: result(zz, 0).wait_send())
            for k in range(1, NCH):
                result(zz, k).wait_send()

    for store in stores:
        store.wait()


def scan_call(norm, q, k, v, g, rates, residue):
    hbm = pl.BlockSpec(memory_space=pltpu.HBM)
    vmem = pl.BlockSpec(memory_space=pltpu.VMEM)
    big = pltpu.VMEM((CHN, ROWS), F32)
    half = pltpu.VMEM((CHN, ROWS), jnp.bfloat16)
    table = pltpu.VMEM((MODES, SUB, ROWS), F32)
    small = pltpu.VMEM((MODES, FG), F32)
    dma = pltpu.SemaphoreType.DMA
    wide = jax.ShapeDtypeStruct((CHN, ROWS), jnp.bfloat16)
    return pl.pallas_call(
        functools.partial(scan_kernel, norm),
        out_shape=(wide, wide, wide, jax.ShapeDtypeStruct((MODES, FG), F32)),
        in_specs=[hbm] * 6,
        out_specs=(hbm, hbm, hbm, vmem),
        scratch_shapes=[
            half, half, half, half, small, small,
            big, big, big, big, half, half, half,
            table, table, table, table,
            pltpu.VMEM((PLANE, 5, SUB, ROWS), F32),
            pltpu.VMEM((PLANE, 5, SUB, ROWS), F32),
            pltpu.VMEM((2, SUB, ROWS), F32),
            pltpu.VMEM((9, SUB, ROWS), F32),
            pltpu.VMEM((NZ, 9, SUB, ROWS), F32),
            pltpu.VMEM((NZ, 8, SUB, ROWS), F32),
            pltpu.VMEM((8, SUB, ROWS), F32),
            pltpu.VMEM((2, 2, ROWS), F32),
            pltpu.VMEM((NCH, 2, 2, ROWS), F32),
            pltpu.VMEM((PLANE, 4, SUB, ROWS), F32),
            pltpu.VMEM((PLANE, 4, SUB, ROWS), F32),
            pltpu.VMEM((2, 2, ROWS), F32),
            pltpu.VMEM((PLANE, 2, 2, ROWS), F32),
            dma((6,)), dma((12,)),
            dma((PLANE - 1,)), dma((PLANE - 1,)), dma, dma((NZ,)), dma((NZ,)), dma,
            dma((NZ * NCH,)), dma((NCH,)),
            dma((PLANE - 1,)), dma((PLANE - 1,)), dma((PLANE - 1,)), dma((PLANE - 1,)),
        ],
        compiler_params=pltpu.CompilerParams(
            collective_id=0, has_side_effects=True, vmem_limit_bytes=63 * 2**20
        ),
        name="scan_states",
    )(q, k, v, g, rates, residue)


def finish_kernel(*refs):
    half = (len(refs) - 2) // 3
    srcs, dsts, held = refs[:half], refs[half : 2 * half], refs[2 * half : 3 * half]
    in_sem, out_sem = refs[3 * half :]
    loads = [pltpu.make_async_copy(srcs[i], held[i], in_sem.at[i]) for i in range(half)]
    stores = [pltpu.make_async_copy(held[i], dsts[i], out_sem.at[i]) for i in range(half)]
    for load in loads:
        load.start()
    for load, store in zip(loads, stores):
        load.wait()
        store.start()
    for store in stores:
        store.wait()


def finish_call(*results):
    n = len(results)
    hbm = pl.BlockSpec(memory_space=pl.ANY)
    return pl.pallas_call(
        finish_kernel,
        out_shape=tuple(jax.ShapeDtypeStruct(r.shape, r.dtype) for r in results),
        in_specs=[hbm] * n,
        out_specs=(hbm,) * n,
        scratch_shapes=[pltpu.VMEM(r.shape, r.dtype) for r in results]
        + [pltpu.SemaphoreType.DMA((n,)), pltpu.SemaphoreType.DMA((n,))],
        name="finish",
    )(*results)


def local(q_branch, k_branch, v_branch, grad_gated, decay_rates, residue):
    norm = 1.0 / math.sqrt(q_branch.shape[1] * lax.axis_size("ctx"))
    grad_q, grad_k, grad_v, res = finish_call(
        *scan_call(norm, q_branch, k_branch, v_branch, grad_gated, decay_rates.T, residue.T)
    )
    return grad_q, grad_k, grad_v, res.T


def solution(mesh):
    in_specs = (P("ch", "ctx"), P("ch", "ctx"), P("ch", "ctx"), P("ch", "ctx"), P(), P())
    out_specs = (P("ch", "ctx"), P("ch", "ctx"), P("ch", "ctx"), P())
    return jax.shard_map(local, mesh=mesh, in_specs=in_specs, out_specs=out_specs, check_vma=False)
```

```python
import functools
import math

import jax
import jax.numpy as jnp
from jax import lax
from jax.experimental import pallas as pl
from jax.experimental.pallas import tpu as pltpu
from jax.sharding import PartitionSpec as P

MESH = pl.DeviceIdType.MESH
F32 = jnp.float32

NX, NZ, NY, NCH = 4, 16, 2, 4
PLANE = NX * NY
MODES = 16
FG = 256
CHN = 1024
ROWS = 128
SUB = 8
GROUP = 8
HOME = 0
ANSWER_FIRST = (1, 2, 3)
ANSWER_LATER = (4, 5, 6, 7, 15, 8, 14, 9, 13, 10, 12, 11)
NEAR = ((0, 1), (0, 3), (1, 0))
FAR = ((1, 2), (1, 1), (1, 3), (0, 2))
PARTS = ((4, 5, 6), (1, 2, 3), (0,))


def tree_sum(terms):
    terms = list(terms)
    while len(terms) > 1:
        terms = [
            terms[i] + terms[i + 1] if i + 1 < len(terms) else terms[i]
            for i in range(0, len(terms), 2)
        ]
    return terms[0]


def scan_kernel(
    norm,
    q_hbm, k_hbm, v_hbm, g_hbm, poles_hbm,
    gq_out, gk_out, gv_out, res_out,
    q_in, k_in, v_in, g_in, poles_in,
    x_kv, x_g, c_out, c_grad,
    d_tab, w_tab, plane_decay_tab, block_decay_tab,
    a_send, a_recv, rows_tmp, b_send, b_recv, owner_out, c_recv, r_send, r_recv, r_sum, e_send, e_recv,
    f_recv, in_sem,
    a_send_sem, a_recv_sem, b_send_sem, b_recv_sem, c_send_sem, c_recv_sem,
    r_send_sem, r_recv_sem, g_send_sem, g_recv_sem, e_send_sem, e_recv_sem, f_send_sem, f_recv_sem,
):
    ctx, ch = lax.axis_index("ctx"), lax.axis_index("ch")
    y, z, x = lax.div(ctx, NX * NZ), lax.rem(lax.div(ctx, NX), NZ), lax.rem(ctx, NX)
    a = y * NX + x
    is_home = z == HOME
    x_plus = [lax.rem(x + k, NX) for k in range(NX)]
    y_plus = [lax.rem(y + k, NY) for k in range(NY)]
    ch_plus = [lax.rem(ch + k, NCH) for k in range(NCH)]
    column = y * (NZ * NX) + x

    plane = [y_plus[dy] * NX + x_plus[dx] for dy, dx in FAR + NEAR]
    plane_ids = [((y_plus[dy] * NZ + z) * NX + x_plus[dx], ch) for dy, dx in FAR + NEAR]

    line_ids = [(plane_ids[i], plane[i]) for i, (dy, dx) in enumerate(FAR + NEAR) if dy == 0]

    def z_id(zz):
        return column + zz * NX, ch

    def cross_id(k, dy):
        return (y_plus[dy] * NZ + HOME) * NX + x, ch_plus[k]

    cross = [(k, dy) for k in range(NCH) for dy in reversed(range(NY)) if k or dy]

    loads = [
        pltpu.make_async_copy(src, dst, in_sem.at[i])
        for i, (src, dst) in enumerate(
            [
                (k_hbm, k_in), (v_hbm, v_in), (g_hbm, g_in), (q_hbm, q_in),
                (poles_hbm, poles_in),
            ]
        )
    ]
    for i in (4, 0, 1, 2, 3):
        loads[i].start()

    barrier = pltpu.get_barrier_semaphore()

    def greet(device):
        pl.semaphore_signal(barrier, inc=1, device_id=device, device_id_type=MESH)

    for device in plane_ids:
        greet(device)

    @pl.when(jnp.logical_not(is_home))
    def _():
        greet(z_id(HOME))

    @pl.when(is_home)
    def _():
        for k, dy in cross:
            if k != 0:
                greet(cross_id(k, dy))

        @pl.loop(1, NZ)
        def _(zz):
            greet(z_id(zz))

    loads[4].wait()
    rate_t = poles_in[0]
    weight_t = poles_in[1] * jnp.sqrt(2.0 * rate_t)
    odd = lax.broadcasted_iota(jnp.int32, (SUB, ROWS), 0) % 2 == 1
    for m in range(MODES):
        rate = jnp.where(odd, rate_t[m : m + 1, ROWS:], rate_t[m : m + 1, :ROWS])
        d_tab[m] = jnp.exp(-rate)
        block_decay_tab[m] = jnp.exp(-rate * ROWS)
        plane_decay_tab[m] = jnp.exp(-rate * (ROWS * NX))
        w_tab[m] = jnp.where(odd, weight_t[m : m + 1, ROWS:], weight_t[m : m + 1, :ROWS])

    loads[0].wait()
    loads[1].wait()
    for j in range(SUB):
        rows = pl.ds(j * ROWS, ROWS)
        product = k_in[rows, :].astype(F32) * v_in[rows, :].astype(F32)
        x_kv[pl.ds(j, ROWS, stride=SUB), :] = product.T
    loads[2].wait()
    loads[3].wait()
    for j in range(SUB):
        rows = pl.ds(j * ROWS, ROWS)
        product = g_in[rows, :].astype(F32) * q_in[rows, :].astype(F32)
        x_g[pl.ds(j, ROWS, stride=SUB), :] = product.T

    def at(t):
        return pl.ds(pl.multiple_of(t * SUB, SUB), SUB)

    zero = jnp.zeros((SUB, ROWS), F32)
    for p in range(PLANE):
        a_send[p, 4] = zero
    for first in range(0, MODES, GROUP):
        modes = range(first, first + GROUP)
        d = [d_tab[m] for m in modes]

        def end_step(t, carry, d=d):
            ahead, back, acc = carry
            here, there = at(t), at(ROWS - 1 - t)
            value, grad, late = x_kv[here, :], x_g[here, :], x_g[there, :]
            ahead = tuple(d[i] * ahead[i] + value for i in range(GROUP))
            back = tuple(d[i] * back[i] + late for i in range(GROUP))
            acc = tuple(acc[i] + grad * ahead[i] for i in range(GROUP))
            return ahead, back, acc

        start = ((zero,) * GROUP,) * 3
        ahead, back, acc = lax.fori_loop(0, ROWS, end_step, start, unroll=4)
        for i, m in enumerate(modes):
            a_send[m // 2, m % 2] = ahead[i]
            a_send[m // 2, 2 + m % 2] = back[i]
            rows = 2 * (m % 2)
            a_send[m // 2, 4, rows : rows + 2, :] = tree_sum(
                acc[i][2 * r : 2 * r + 2, :] for r in range(4)
            )

    beyond = jnp.where(is_home, (NCH - 1) * NY + NZ - 1, 1)
    pl.semaphore_wait(barrier, len(plane) + beyond)

    def remote(src, dst, send_sem, recv_sem, device):
        return pltpu.make_async_remote_copy(
            src_ref=src, dst_ref=dst, send_sem=send_sem, recv_sem=recv_sem,
            device_id=device, device_id_type=MESH,
        )

    a_copies = [
        remote(a_send.at[p], a_recv.at[a], a_send_sem.at[i], a_recv_sem.at[i], device)
        for i, (p, device) in enumerate(zip(plane, plane_ids))
    ]
    for copy in a_copies:
        copy.start()
    a_recv[a] = a_send[a]

    for first in range(0, MODES, GROUP):
        modes = range(first, first + GROUP)
        d = [d_tab[m] for m in modes]
        w = [w_tab[m] for m in modes]

        def local_step(t, carry, d=d, w=w, first=first):
            ahead, back = carry
            here, there = at(t), at(ROWS - 1 - t)
            value, late = x_kv[here, :], x_g[there, :]
            ahead = tuple(d[i] * ahead[i] + value for i in range(GROUP))
            back = tuple(d[i] * back[i] + late for i in range(GROUP))
            out = tree_sum(w[i] * ahead[i] for i in range(GROUP))
            out_grad = tree_sum(w[i] * back[i] for i in range(GROUP))
            if first:
                out = out + c_out[here, :]
                out_grad = out_grad + c_grad[there, :]
            c_out[here, :] = out
            c_grad[there, :] = out_grad
            return ahead, back

        lax.fori_loop(0, ROWS, local_step, ((zero,) * GROUP,) * 2, unroll=4)

    mine = pl.ds(2 * a, 2)
    d2, block_decay, plane_decay = d_tab[mine], block_decay_tab[mine], plane_decay_tab[mine]
    for copy in a_copies:
        copy.wait_recv()

    def over_repeats(value):
        rows_tmp[...] = value
        return [tree_sum(rows_tmp[i, 2 * r : 2 * r + 2, :] for r in range(4)) for i in range(2)]

    between = jnp.zeros((2, SUB, ROWS), F32)
    for yy in range(NY):
        run = jnp.zeros((2, SUB, ROWS), F32)
        for xx in range(NX):
            slot = yy * NX + xx
            between = between + d2 * a_recv[slot, 2:4] * run
            run = block_decay * run + a_recv[slot, 0:2]
        b_send[2 * yy : 2 * yy + 2] = run
        run = jnp.zeros((2, SUB, ROWS), F32)
        for xx in reversed(range(NX)):
            run = block_decay * run + a_recv[yy * NX + xx, 2:4]
        b_send[4 + 2 * yy : 6 + 2 * yy] = run
    b_send[8] = tree_sum(a_recv[slot, 4] for slot in range(PLANE))
    for i, rows in enumerate(over_repeats(between)):
        b_send[8, 2 * i : 2 * i + 2, :] = b_send[8, 2 * i : 2 * i + 2, :] + rows

    def to_home(zz):
        return remote(b_send, b_recv.at[zz], b_send_sem, b_recv_sem.at[zz], z_id(HOME))

    def answer(zz):
        return remote(owner_out.at[zz], c_recv, c_send_sem.at[zz], c_recv_sem, z_id(zz))

    def result(k, dy):
        return remote(
            r_send, r_recv.at[ch, y], r_send_sem.at[k, dy], r_recv_sem.at[k, dy], cross_id(k, dy)
        )

    def summed(zz):
        return remote(r_sum, r_sum, g_send_sem.at[zz], g_recv_sem, z_id(zz))

    @pl.when(jnp.logical_not(is_home))
    def _():
        to_home(z).start()

    @pl.when(is_home)
    def _():
        b_recv[HOME] = b_send[...]
        for zz in range(NZ):
            if zz != HOME:
                to_home(zz).wait_recv()
        run = jnp.zeros((2, SUB, ROWS), F32)
        between = jnp.zeros((2, SUB, ROWS), F32)
        for yy in range(NY):
            for zz in range(NZ):
                owner_out[zz, 2 * yy : 2 * yy + 2] = run
                between = between + d2 * b_recv[zz, 4 + 2 * yy : 6 + 2 * yy] * run
                run = plane_decay * run + b_recv[zz, 2 * yy : 2 * yy + 2]
        within = tree_sum(b_recv[zz, 8] for zz in range(NZ))
        for i, rows in enumerate(over_repeats(between)):
            r_send[i] = rows + within[2 * i : 2 * i + 2, :]
        for k, dy in cross:
            result(k, dy).start()
        run = jnp.zeros((2, SUB, ROWS), F32)
        for yy in reversed(range(NY)):
            for zz in reversed(range(NZ)):
                owner_out[zz, 4 + 2 * yy : 6 + 2 * yy] = run
                run = plane_decay * run + b_recv[zz, 4 + 2 * yy : 6 + 2 * yy]
        for zz in ANSWER_FIRST:
            answer(zz).start()
        r_recv[ch, y] = r_send[...]
        c_recv[...] = owner_out[HOME]

    @pl.when(jnp.logical_not(is_home))
    def _():
        answer(z).wait_recv()

    for yy in range(NY):
        run = c_recv[2 * yy : 2 * yy + 2]
        for xx in range(NX):
            slot = yy * NX + xx
            e_send[slot, 0:2] = run
            run = block_decay * run + a_recv[slot, 0:2]
        run = c_recv[4 + 2 * yy : 6 + 2 * yy]
        for xx in reversed(range(NX)):
            slot = yy * NX + xx
            e_send[slot, 2:4] = run
            run = block_decay * run + a_recv[slot, 2:4]
    e_copies = [
        remote(e_send.at[p], e_recv.at[a], e_send_sem.at[i], e_recv_sem.at[i], device)
        for i, (p, device) in enumerate(zip(plane, plane_ids))
    ]
    for copy in e_copies:
        copy.start()
    e_recv[a] = e_send[a]

    @pl.when(is_home)
    def _():
        for zz in ANSWER_LATER:
            answer(zz).start()

    @pl.when(is_home)
    def _():
        for k, dy in cross:
            result(k, dy).wait_recv()
        r_sum[...] = (r_recv[0] + r_recv[1]) + (r_recv[2] + r_recv[3])
        for zz in ANSWER_FIRST + ANSWER_LATER:
            summed(zz).start()

    pl.when(jnp.logical_not(is_home))(summed(z).wait_recv)
    f_copies = [
        remote(r_sum, f_recv.at[x], f_send_sem.at[i], f_recv_sem.at[i], device)
        for i, (device, _) in enumerate(line_ids)
    ]
    for copy in f_copies:
        copy.start()
    f_recv[x] = r_sum[...]

    for members in PARTS:
        for n in members:
            e_copies[n].wait_recv()
        slots = [plane[n] for n in members] + ([a] if members == PARTS[0] else [])
        pairs = [(slot, i) for slot in slots for i in range(2)]
        d = [d_tab[2 * slot + i] for slot, i in pairs]
        w = [w_tab[2 * slot + i] for slot, i in pairs]
        ahead = tuple(w[n] * e_recv[slot, i] for n, (slot, i) in enumerate(pairs))
        back = tuple(w[n] * e_recv[slot, 2 + i] for n, (slot, i) in enumerate(pairs))

        def carry_step(t, carry, d=d):
            ahead, back = carry
            here, there = at(t), at(ROWS - 1 - t)
            ahead = tuple(d[n] * ahead[n] for n in range(len(d)))
            back = tuple(d[n] * back[n] for n in range(len(d)))
            c_out[here, :] = c_out[here, :] + tree_sum(ahead)
            c_grad[there, :] = c_grad[there, :] + tree_sum(back)
            return ahead, back

        lax.fori_loop(0, ROWS, carry_step, (ahead, back), unroll=4)

    for j in range(SUB):
        rows = pl.ds(j * ROWS, ROWS)
        lanes = pl.ds(j, ROWS, stride=SUB)
        gq_out[rows, :] = (g_in[rows, :].astype(F32) * c_out[lanes, :].T).astype(jnp.bfloat16)
        conv_grad = c_grad[lanes, :].T
        gk_out[rows, :] = (conv_grad * v_in[rows, :].astype(F32)).astype(jnp.bfloat16)
        gv_out[rows, :] = (conv_grad * k_in[rows, :].astype(F32)).astype(jnp.bfloat16)

    for copy in f_copies:
        copy.wait_recv()
    for m in range(MODES):
        for half in range(2):
            cols = slice(half * ROWS, (half + 1) * ROWS)
            res_out[m : m + 1, cols] = f_recv[m // 2 % NX, m // 2 // NX, m % 2, half : half + 1, :]
    res_out[...] = res_out[...] * (jnp.sqrt(2.0 * poles_in[0]) * norm)
    for copy in a_copies + e_copies + f_copies:
        copy.wait_send()
    @pl.when(jnp.logical_not(is_home))
    def _():
        to_home(z).wait_send()

    @pl.when(is_home)
    def _():
        @pl.loop(1, NZ)
        def _(zz):
            answer(zz).wait_send()

        for k, dy in cross:
            result(k, dy).wait_send()

        @pl.loop(1, NZ)
        def _(zz):
            summed(zz).wait_send()


def scan_call(norm, q, k, v, g, poles):
    hbm = pl.BlockSpec(memory_space=pltpu.HBM)
    big = pltpu.VMEM((CHN, ROWS), F32)
    half = pltpu.VMEM((CHN, ROWS), jnp.bfloat16)
    table = pltpu.VMEM((MODES, SUB, ROWS), F32)
    dma = pltpu.SemaphoreType.DMA
    wide = jax.ShapeDtypeStruct((CHN, ROWS), jnp.bfloat16)
    return pl.pallas_call(
        functools.partial(scan_kernel, norm),
        out_shape=(wide, wide, wide, jax.ShapeDtypeStruct((MODES, FG), F32)),
        in_specs=[hbm] * 5,
        out_specs=(pl.BlockSpec(memory_space=pltpu.VMEM),) * 4,
        scratch_shapes=[
            half, half, half, half, pltpu.VMEM((2, MODES, FG), F32),
            big, big, big, big,
            table, table, table, table,
            pltpu.VMEM((PLANE, 5, SUB, ROWS), F32),
            pltpu.VMEM((PLANE, 5, SUB, ROWS), F32),
            pltpu.VMEM((2, SUB, ROWS), F32),
            pltpu.VMEM((9, SUB, ROWS), F32),
            pltpu.VMEM((NZ, 9, SUB, ROWS), F32),
            pltpu.VMEM((NZ, 8, SUB, ROWS), F32),
            pltpu.VMEM((8, SUB, ROWS), F32),
            pltpu.VMEM((2, 2, ROWS), F32),
            pltpu.VMEM((NCH, NY, 2, 2, ROWS), F32),
            pltpu.VMEM((NY, 2, 2, ROWS), F32),
            pltpu.VMEM((PLANE, 4, SUB, ROWS), F32),
            pltpu.VMEM((PLANE, 4, SUB, ROWS), F32),
            pltpu.VMEM((NX, NY, 2, 2, ROWS), F32),
            dma((5,)),
            dma((PLANE - 1,)), dma((PLANE - 1,)), dma, dma((NZ,)), dma((NZ,)), dma,
            dma((NCH, NY)), dma((NCH, NY)), dma((NZ,)), dma,
            dma((PLANE - 1,)), dma((PLANE - 1,)), dma((NX - 1,)), dma((NX - 1,)),
        ],
        compiler_params=pltpu.CompilerParams(
            collective_id=0, has_side_effects=True, vmem_limit_bytes=54336 * 2**10
        ),
        name="scan_states",
    )(q, k, v, g, poles)


def finish_kernel(*refs):
    half = len(refs) // 2
    srcs, dsts, sems = refs[:half], refs[half : 2 * half], refs[2 * half]
    copies = [pltpu.make_async_copy(srcs[i], dsts[i], sems.at[i]) for i in range(half)]
    for copy in copies:
        copy.start()
    for copy in copies:
        copy.wait()


def finish_call(*results):
    n = len(results)
    anywhere = pl.BlockSpec(memory_space=pl.ANY)
    return pl.pallas_call(
        finish_kernel,
        out_shape=tuple(jax.ShapeDtypeStruct(r.shape, r.dtype) for r in results),
        in_specs=[anywhere] * n,
        out_specs=(anywhere,) * n,
        scratch_shapes=[pltpu.SemaphoreType.DMA((n,))],
        compiler_params=pltpu.CompilerParams(vmem_limit_bytes=4 * 2**20),
        name="finish",
    )(*results)


def local(q_branch, k_branch, v_branch, grad_gated, decay_rates, residue):
    norm = 1.0 / math.sqrt(q_branch.shape[1] * lax.axis_size("ctx"))
    poles = jnp.stack([decay_rates.T, residue.T])
    grad_q, grad_k, grad_v, res = finish_call(
        *scan_call(norm, q_branch, k_branch, v_branch, grad_gated, poles)
    )
    return grad_q, grad_k, grad_v, res.T


def solution(mesh):
    in_specs = (P("ch", "ctx"), P("ch", "ctx"), P("ch", "ctx"), P("ch", "ctx"), P(), P())
    out_specs = (P("ch", "ctx"), P("ch", "ctx"), P("ch", "ctx"), P())
    return jax.shard_map(local, mesh=mesh, in_specs=in_specs, out_specs=out_specs, check_vma=False)
```

```python
import functools
import math

import jax
import jax.numpy as jnp
from jax import lax
from jax.experimental import pallas as pl
from jax.experimental.pallas import tpu as pltpu
from jax.sharding import PartitionSpec as P

MESH = pl.DeviceIdType.MESH
F32 = jnp.float32

NX, NZ, NY, NCH = 4, 16, 2, 4
PLANE = NX * NY
MODES = 16
FG = 256
CHN = 1024
ROWS = 128
SUB = 8
GROUP = 8
HOME = 0
ANSWER_FIRST = (1, 2, 3, 4, 5, 6, 7, 8)
ANSWER_LATER = (9, 15, 10, 14, 11, 13, 12)
DIRECT = 5
ALONG = (2, 1, 3)
NEAR = ((0, 1), (0, 3), (1, 0))
FAR = ((1, 2), (1, 1), (1, 3), (0, 2))


def tree_sum(terms):
    terms = list(terms)
    while len(terms) > 1:
        terms = [
            terms[i] + terms[i + 1] if i + 1 < len(terms) else terms[i]
            for i in range(0, len(terms), 2)
        ]
    return terms[0]


def scan_kernel(
    norm,
    q_hbm, k_hbm, v_hbm, g_hbm, poles_hbm,
    gq_out, gk_out, gv_out, res_out,
    q_in, k_in, v_in, g_in, poles_in,
    x_kv, x_g, c_out, c_grad,
    d_tab, w_tab, plane_decay_tab, block_decay_tab,
    a_send, a_recv, rows_tmp, b_send, b_recv, owner_out, c_recv, r_send, r_recv, r_sum, e_send, e_recv,
    f_recv, in_sem,
    a_send_sem, a_recv_sem, b_send_sem, b_recv_sem, c_send_sem, c_recv_sem,
    r_send_sem, r_recv_sem, g_send_sem, g_recv_sem, e_send_sem, e_recv_sem, f_send_sem, f_recv_sem,
):
    ctx, ch = lax.axis_index("ctx"), lax.axis_index("ch")
    y, z, x = lax.div(ctx, NX * NZ), lax.rem(lax.div(ctx, NX), NZ), lax.rem(ctx, NX)
    a = y * NX + x
    is_home = z == HOME
    is_direct = z < DIRECT
    x_plus = [lax.rem(x + k, NX) for k in range(NX)]
    y_plus = [lax.rem(y + k, NY) for k in range(NY)]
    ch_plus = [lax.rem(ch + k, NCH) for k in range(NCH)]
    column = y * (NZ * NX) + x

    plane = [y_plus[dy] * NX + x_plus[dx] for dy, dx in FAR + NEAR]
    plane_ids = [((y_plus[dy] * NZ + z) * NX + x_plus[dx], ch) for dy, dx in FAR + NEAR]

    def line_id(zz, k):
        return (y * NZ + zz) * NX + x_plus[k], ch

    def z_id(zz):
        return column + zz * NX, ch

    def cross_id(k, dy):
        return (y_plus[dy] * NZ + HOME) * NX + x, ch_plus[k]

    cross = [(k, dy) for k in range(NCH) for dy in reversed(range(NY)) if k or dy]

    loads = [
        pltpu.make_async_copy(src, dst, in_sem.at[i])
        for i, (src, dst) in enumerate(
            [
                (k_hbm, k_in), (v_hbm, v_in), (g_hbm, g_in), (q_hbm, q_in),
                (poles_hbm, poles_in),
            ]
        )
    ]
    for i in (4, 0, 1, 2, 3):
        loads[i].start()

    barrier = pltpu.get_barrier_semaphore()

    def greet(device):
        pl.semaphore_signal(barrier, inc=1, device_id=device, device_id_type=MESH)

    for device in plane_ids:
        greet(device)

    @pl.when(jnp.logical_not(is_home))
    def _():
        greet(z_id(HOME))

    @pl.when(jnp.logical_and(is_direct, jnp.logical_not(is_home)))
    def _():
        for k in ALONG:
            greet(line_id(HOME, k))

    @pl.when(is_home)
    def _():
        for k, dy in cross:
            if k != 0:
                greet(cross_id(k, dy))

        @pl.loop(1, NZ)
        def _(zz):
            greet(z_id(zz))

        @pl.loop(1, DIRECT)
        def _(zz):
            for k in ALONG:
                greet(line_id(zz, k))

    loads[4].wait()
    rate_t = poles_in[0]
    weight_t = poles_in[1] * jnp.sqrt(2.0 * rate_t)
    odd = lax.broadcasted_iota(jnp.int32, (SUB, ROWS), 0) % 2 == 1
    for m in range(MODES):
        rate = jnp.where(odd, rate_t[m : m + 1, ROWS:], rate_t[m : m + 1, :ROWS])
        d_tab[m] = jnp.exp(-rate)
        block_decay_tab[m] = jnp.exp(-rate * ROWS)
        plane_decay_tab[m] = jnp.exp(-rate * (ROWS * NX))
        w_tab[m] = jnp.where(odd, weight_t[m : m + 1, ROWS:], weight_t[m : m + 1, :ROWS])

    loads[0].wait()
    loads[1].wait()
    for j in range(SUB):
        rows = pl.ds(j * ROWS, ROWS)
        product = k_in[rows, :].astype(F32) * v_in[rows, :].astype(F32)
        x_kv[pl.ds(j, ROWS, stride=SUB), :] = product.T
    loads[2].wait()
    loads[3].wait()
    for j in range(SUB):
        rows = pl.ds(j * ROWS, ROWS)
        product = g_in[rows, :].astype(F32) * q_in[rows, :].astype(F32)
        x_g[pl.ds(j, ROWS, stride=SUB), :] = product.T

    def at(t):
        return pl.ds(pl.multiple_of(t * SUB, SUB), SUB)

    zero = jnp.zeros((SUB, ROWS), F32)
    for p in range(PLANE):
        a_send[p, 4] = zero
    for first in range(0, MODES, GROUP):
        modes = range(first, first + GROUP)
        d = [d_tab[m] for m in modes]

        def end_step(t, carry, d=d):
            ahead, back, acc = carry
            here, there = at(t), at(ROWS - 1 - t)
            value, grad, late = x_kv[here, :], x_g[here, :], x_g[there, :]
            ahead = tuple(d[i] * ahead[i] + value for i in range(GROUP))
            back = tuple(d[i] * back[i] + late for i in range(GROUP))
            acc = tuple(acc[i] + grad * ahead[i] for i in range(GROUP))
            return ahead, back, acc

        start = ((zero,) * GROUP,) * 3
        ahead, back, acc = lax.fori_loop(0, ROWS, end_step, start, unroll=16)
        for i, m in enumerate(modes):
            a_send[m // 2, m % 2] = ahead[i]
            a_send[m // 2, 2 + m % 2] = back[i]
            rows = 2 * (m % 2)
            a_send[m // 2, 4, rows : rows + 2, :] = tree_sum(
                acc[i][2 * r : 2 * r + 2, :] for r in range(4)
            )

    at_home = (NCH - 1) * NY + NZ - 1 + (DIRECT - 1) * len(ALONG)
    beyond = jnp.where(is_home, at_home, jnp.where(is_direct, NX, 1))
    pl.semaphore_wait(barrier, len(plane) + beyond)

    def remote(src, dst, send_sem, recv_sem, device):
        return pltpu.make_async_remote_copy(
            src_ref=src, dst_ref=dst, send_sem=send_sem, recv_sem=recv_sem,
            device_id=device, device_id_type=MESH,
        )

    a_copies = [
        remote(a_send.at[p], a_recv.at[a], a_send_sem.at[i], a_recv_sem.at[i], device)
        for i, (p, device) in enumerate(zip(plane, plane_ids))
    ]
    for copy in a_copies:
        copy.start()
    a_recv[a] = a_send[a]

    for first in range(0, MODES, GROUP):
        modes = range(first, first + GROUP)
        d = [d_tab[m] for m in modes]
        w = [w_tab[m] for m in modes]

        def local_step(t, carry, d=d, w=w, first=first):
            ahead, back = carry
            here, there = at(t), at(ROWS - 1 - t)
            value, late = x_kv[here, :], x_g[there, :]
            ahead = tuple(d[i] * ahead[i] + value for i in range(GROUP))
            back = tuple(d[i] * back[i] + late for i in range(GROUP))
            out = tree_sum(w[i] * ahead[i] for i in range(GROUP))
            out_grad = tree_sum(w[i] * back[i] for i in range(GROUP))
            if first:
                out = out + c_out[here, :]
                out_grad = out_grad + c_grad[there, :]
            c_out[here, :] = out
            c_grad[there, :] = out_grad
            return ahead, back

        lax.fori_loop(0, ROWS, local_step, ((zero,) * GROUP,) * 2, unroll=16)

    mine = pl.ds(2 * a, 2)
    d2, block_decay, plane_decay = d_tab[mine], block_decay_tab[mine], plane_decay_tab[mine]
    for copy in a_copies:
        copy.wait_recv()

    def over_repeats(value):
        rows_tmp[...] = value
        return [tree_sum(rows_tmp[i, 2 * r : 2 * r + 2, :] for r in range(4)) for i in range(2)]

    between = jnp.zeros((2, SUB, ROWS), F32)
    for yy in range(NY):
        run = jnp.zeros((2, SUB, ROWS), F32)
        for xx in range(NX):
            slot = yy * NX + xx
            between = between + d2 * a_recv[slot, 2:4] * run
            run = block_decay * run + a_recv[slot, 0:2]
        b_send[2 * yy : 2 * yy + 2] = run
        run = jnp.zeros((2, SUB, ROWS), F32)
        for xx in reversed(range(NX)):
            run = block_decay * run + a_recv[yy * NX + xx, 2:4]
        b_send[4 + 2 * yy : 6 + 2 * yy] = run
    b_send[8] = tree_sum(a_recv[slot, 4] for slot in range(PLANE))
    for i, rows in enumerate(over_repeats(between)):
        b_send[8, 2 * i : 2 * i + 2, :] = b_send[8, 2 * i : 2 * i + 2, :] + rows

    def to_home(zz):
        return remote(b_send, b_recv.at[zz], b_send_sem, b_recv_sem.at[zz], z_id(HOME))

    def answer(zz):
        return remote(owner_out.at[zz], c_recv, c_send_sem.at[zz], c_recv_sem, z_id(zz))

    def result(k, dy):
        return remote(
            r_send, r_recv.at[ch, y], r_send_sem.at[k, dy], r_recv_sem.at[k, dy], cross_id(k, dy)
        )

    def summed(zz):
        return remote(r_sum, r_sum, g_send_sem.at[zz], g_recv_sem, z_id(zz))

    def along(zz, k):
        return remote(
            r_sum, f_recv.at[x], f_send_sem.at[zz, k], f_recv_sem.at[k], line_id(zz, k)
        )

    def pass_on():
        for k in ALONG:
            along(z, k).start()
        f_recv[x] = r_sum[...]

    @pl.when(jnp.logical_not(is_home))
    def _():
        to_home(z).start()

    @pl.when(is_home)
    def _():
        b_recv[HOME] = b_send[...]
        for zz in range(NZ):
            if zz != HOME:
                to_home(zz).wait_recv()
        run = jnp.zeros((2, SUB, ROWS), F32)
        between = jnp.zeros((2, SUB, ROWS), F32)
        for yy in range(NY):
            for zz in range(NZ):
                owner_out[zz, 2 * yy : 2 * yy + 2] = run
                between = between + d2 * b_recv[zz, 4 + 2 * yy : 6 + 2 * yy] * run
                run = plane_decay * run + b_recv[zz, 2 * yy : 2 * yy + 2]
        within = tree_sum(b_recv[zz, 8] for zz in range(NZ))
        for i, rows in enumerate(over_repeats(between)):
            r_send[i] = rows + within[2 * i : 2 * i + 2, :]
        for k, dy in cross:
            result(k, dy).start()
        run = jnp.zeros((2, SUB, ROWS), F32)
        for yy in reversed(range(NY)):
            for zz in reversed(range(NZ)):
                owner_out[zz, 4 + 2 * yy : 6 + 2 * yy] = run
                run = plane_decay * run + b_recv[zz, 4 + 2 * yy : 6 + 2 * yy]
        for zz in ANSWER_FIRST:
            answer(zz).start()
        r_recv[ch, y] = r_send[...]
        c_recv[...] = owner_out[HOME]

    @pl.when(jnp.logical_not(is_home))
    def _():
        answer(z).wait_recv()

    for yy in range(NY):
        run = c_recv[2 * yy : 2 * yy + 2]
        for xx in range(NX):
            slot = yy * NX + xx
            e_send[slot, 0:2] = run
            run = block_decay * run + a_recv[slot, 0:2]
        run = c_recv[4 + 2 * yy : 6 + 2 * yy]
        for xx in reversed(range(NX)):
            slot = yy * NX + xx
            e_send[slot, 2:4] = run
            run = block_decay * run + a_recv[slot, 2:4]
    e_copies = [
        remote(e_send.at[p], e_recv.at[a], e_send_sem.at[i], e_recv_sem.at[i], device)
        for i, (p, device) in enumerate(zip(plane, plane_ids))
    ]
    for copy in e_copies:
        copy.start()
    e_recv[a] = e_send[a]

    @pl.when(is_home)
    def _():
        for zz in ANSWER_LATER:
            answer(zz).start()

    @pl.when(is_home)
    def _():
        for k, dy in cross:
            result(k, dy).wait_recv()
        r_sum[...] = (r_recv[0] + r_recv[1]) + (r_recv[2] + r_recv[3])
        for zz in range(1, DIRECT):
            for k in ALONG + (0,):
                along(zz, k).start()
        pass_on()
        for zz in ANSWER_FIRST + ANSWER_LATER:
            if zz >= DIRECT:
                summed(zz).start()

    @pl.when(jnp.logical_not(is_direct))
    def _():
        summed(z).wait_recv()
        pass_on()

    for copy in e_copies:
        copy.wait_recv()
    d = [d_tab[m] for m in range(MODES)]
    w = [w_tab[m] for m in range(MODES)]
    ahead = tuple(w[m] * e_recv[m // 2, m % 2] for m in range(MODES))
    back = tuple(w[m] * e_recv[m // 2, 2 + m % 2] for m in range(MODES))

    def carry_step(t, carry):
        ahead, back = carry
        here, there = at(t), at(ROWS - 1 - t)
        ahead = tuple(d[n] * ahead[n] for n in range(len(d)))
        back = tuple(d[n] * back[n] for n in range(len(d)))
        c_out[here, :] = c_out[here, :] + tree_sum(ahead)
        c_grad[there, :] = c_grad[there, :] + tree_sum(back)
        return ahead, back

    lax.fori_loop(0, ROWS, carry_step, (ahead, back), unroll=16)

    for j in range(SUB):
        rows = pl.ds(j * ROWS, ROWS)
        lanes = pl.ds(j, ROWS, stride=SUB)
        gq_out[rows, :] = (g_in[rows, :].astype(F32) * c_out[lanes, :].T).astype(jnp.bfloat16)
        conv_grad = c_grad[lanes, :].T
        gk_out[rows, :] = (conv_grad * v_in[rows, :].astype(F32)).astype(jnp.bfloat16)
        gv_out[rows, :] = (conv_grad * k_in[rows, :].astype(F32)).astype(jnp.bfloat16)

    for k in ALONG:
        along(z, k).wait_recv()
    pl.when(jnp.logical_and(is_direct, jnp.logical_not(is_home)))(along(z, 0).wait_recv)
    for m in range(MODES):
        for half in range(2):
            cols = slice(half * ROWS, (half + 1) * ROWS)
            res_out[m : m + 1, cols] = f_recv[m // 2 % NX, m // 2 // NX, m % 2, half : half + 1, :]
    res_out[...] = res_out[...] * (jnp.sqrt(2.0 * poles_in[0]) * norm)
    for copy in a_copies + e_copies:
        copy.wait_send()
    @pl.when(jnp.logical_not(is_home))
    def _():
        to_home(z).wait_send()

    @pl.when(is_home)
    def _():
        @pl.loop(1, NZ)
        def _(zz):
            answer(zz).wait_send()

        for k, dy in cross:
            result(k, dy).wait_send()

        @pl.loop(1, DIRECT)
        def _(zz):
            for k in range(NX):
                along(zz, k).wait_send()

        @pl.loop(DIRECT, NZ)
        def _(zz):
            summed(zz).wait_send()

    @pl.when(jnp.logical_or(is_home, jnp.logical_not(is_direct)))
    def _():
        for k in ALONG:
            along(z, k).wait_send()


def scan_call(norm, q, k, v, g, poles):
    hbm = pl.BlockSpec(memory_space=pltpu.HBM)
    big = pltpu.VMEM((CHN, ROWS), F32)
    half = pltpu.VMEM((CHN, ROWS), jnp.bfloat16)
    table = pltpu.VMEM((MODES, SUB, ROWS), F32)
    dma = pltpu.SemaphoreType.DMA
    wide = jax.ShapeDtypeStruct((CHN, ROWS), jnp.bfloat16)
    return pl.pallas_call(
        functools.partial(scan_kernel, norm),
        out_shape=(wide, wide, wide, jax.ShapeDtypeStruct((MODES, FG), F32)),
        in_specs=[hbm] * 5,
        out_specs=(pl.BlockSpec(memory_space=pltpu.VMEM),) * 4,
        scratch_shapes=[
            half, half, half, half, pltpu.VMEM((2, MODES, FG), F32),
            big, big, big, big,
            table, table, table, table,
            pltpu.VMEM((PLANE, 5, SUB, ROWS), F32),
            pltpu.VMEM((PLANE, 5, SUB, ROWS), F32),
            pltpu.VMEM((2, SUB, ROWS), F32),
            pltpu.VMEM((9, SUB, ROWS), F32),
            pltpu.VMEM((NZ, 9, SUB, ROWS), F32),
            pltpu.VMEM((NZ, 8, SUB, ROWS), F32),
            pltpu.VMEM((8, SUB, ROWS), F32),
            pltpu.VMEM((2, 2, ROWS), F32),
            pltpu.VMEM((NCH, NY, 2, 2, ROWS), F32),
            pltpu.VMEM((NY, 2, 2, ROWS), F32),
            pltpu.VMEM((PLANE, 4, SUB, ROWS), F32),
            pltpu.VMEM((PLANE, 4, SUB, ROWS), F32),
            pltpu.VMEM((NX, NY, 2, 2, ROWS), F32),
            dma((5,)),
            dma((PLANE - 1,)), dma((PLANE - 1,)), dma, dma((NZ,)), dma((NZ,)), dma,
            dma((NCH, NY)), dma((NCH, NY)), dma((NZ,)), dma,
            dma((PLANE - 1,)), dma((PLANE - 1,)), dma((NZ, NX)), dma((NX,)),
        ],
        compiler_params=pltpu.CompilerParams(
            collective_id=0, has_side_effects=True, vmem_limit_bytes=54336 * 2**10
        ),
        name="scan_states",
    )(q, k, v, g, poles)


def finish_kernel(*refs):
    half = len(refs) // 2
    srcs, dsts, sems = refs[:half], refs[half : 2 * half], refs[2 * half]
    copies = [pltpu.make_async_copy(srcs[i], dsts[i], sems.at[i]) for i in range(half)]
    for copy in copies:
        copy.start()
    for copy in copies:
        copy.wait()


def finish_call(*results):
    n = len(results)
    anywhere = pl.BlockSpec(memory_space=pl.ANY)
    return pl.pallas_call(
        finish_kernel,
        out_shape=tuple(jax.ShapeDtypeStruct(r.shape, r.dtype) for r in results),
        in_specs=[anywhere] * n,
        out_specs=(anywhere,) * n,
        scratch_shapes=[pltpu.SemaphoreType.DMA((n,))],
        compiler_params=pltpu.CompilerParams(vmem_limit_bytes=4 * 2**20),
        name="finish",
    )(*results)


def local(q_branch, k_branch, v_branch, grad_gated, decay_rates, residue):
    norm = 1.0 / math.sqrt(q_branch.shape[1] * lax.axis_size("ctx"))
    poles = jnp.stack([decay_rates.T, residue.T])
    grad_q, grad_k, grad_v, res = finish_call(
        *scan_call(norm, q_branch, k_branch, v_branch, grad_gated, poles)
    )
    return grad_q, grad_k, grad_v, res.T


def solution(mesh):
    in_specs = (P("ch", "ctx"), P("ch", "ctx"), P("ch", "ctx"), P("ch", "ctx"), P(), P())
    out_specs = (P("ch", "ctx"), P("ch", "ctx"), P("ch", "ctx"), P())
    return jax.shard_map(local, mesh=mesh, in_specs=in_specs, out_specs=out_specs, check_vma=False)
```

```python
import functools
import math

import jax
import jax.numpy as jnp
from jax import lax
from jax.experimental import pallas as pl
from jax.experimental.pallas import tpu as pltpu
from jax.sharding import PartitionSpec as P

MESH = pl.DeviceIdType.MESH
F32 = jnp.float32

NX, NZ, NY, NCH = 4, 16, 2, 4
PLANE = NX * NY
MODES = 16
FG = 256
CHN = 1024
ROWS = 128
SUB = 8
GROUP = 8
HOME = 0
ANSWER_FIRST = (1, 2, 3, 4, 5, 6, 7, 8)
ANSWER_LATER = (9, 15, 10, 14, 11, 13, 12)
DIRECT = 5
RESULT_ORDER = (1, 2, 5, 6, 7, 8, 0, 3, 4, 9, 10, 11, 12, 13, 14, 15)
ALONG = (2, 1, 3)
NEAR = ((0, 1), (0, 3), (1, 0))
FAR = ((1, 2), (1, 1), (1, 3), (0, 2))


def tree_sum(terms):
    terms = list(terms)
    while len(terms) > 1:
        terms = [
            terms[i] + terms[i + 1] if i + 1 < len(terms) else terms[i]
            for i in range(0, len(terms), 2)
        ]
    return terms[0]


def scan_kernel(
    norm,
    q_hbm, k_hbm, v_hbm, g_hbm, poles_hbm,
    gq_out, gk_out, gv_out, res_out,
    q_in, k_in, v_in, g_in, poles_in,
    x_kv, x_g, c_out, c_grad,
    d_tab, w_tab, plane_decay_tab, block_decay_tab,
    a_send, a_recv, rows_tmp, b_send, b_recv, owner_out, c_recv, r_send, r_recv, r_sum, e_send, e_recv,
    f_recv, in_sem,
    a_send_sem, a_recv_sem, b_send_sem, b_recv_sem, c_send_sem, c_recv_sem,
    r_send_sem, r_recv_sem, g_send_sem, g_recv_sem, e_send_sem, e_recv_sem, f_send_sem, f_recv_sem,
):
    ctx, ch = lax.axis_index("ctx"), lax.axis_index("ch")
    y, z, x = lax.div(ctx, NX * NZ), lax.rem(lax.div(ctx, NX), NZ), lax.rem(ctx, NX)
    a = y * NX + x
    is_home = z == HOME
    is_direct = z < DIRECT
    x_plus = [lax.rem(x + k, NX) for k in range(NX)]
    y_plus = [lax.rem(y + k, NY) for k in range(NY)]
    ch_plus = [lax.rem(ch + k, NCH) for k in range(NCH)]
    column = y * (NZ * NX) + x

    plane = [y_plus[dy] * NX + x_plus[dx] for dy, dx in FAR + NEAR]
    plane_ids = [((y_plus[dy] * NZ + z) * NX + x_plus[dx], ch) for dy, dx in FAR + NEAR]

    def line_id(zz, k):
        return (y * NZ + zz) * NX + x_plus[k], ch

    def z_id(zz):
        return column + zz * NX, ch

    def cross_id(k, dy):
        return (y_plus[dy] * NZ + HOME) * NX + x, ch_plus[k]

    cross = [(k, dy) for k in range(NCH) for dy in reversed(range(NY)) if k or dy]

    loads = [
        pltpu.make_async_copy(src, dst, in_sem.at[i])
        for i, (src, dst) in enumerate(
            [
                (k_hbm, k_in), (v_hbm, v_in), (g_hbm, g_in), (q_hbm, q_in),
                (poles_hbm, poles_in),
            ]
        )
    ]
    for i in (4, 0, 1, 2, 3):
        loads[i].start()

    barrier = pltpu.get_barrier_semaphore()

    def greet(device):
        pl.semaphore_signal(barrier, inc=1, device_id=device, device_id_type=MESH)

    for device in plane_ids:
        greet(device)

    @pl.when(jnp.logical_not(is_home))
    def _():
        greet(z_id(HOME))

    @pl.when(jnp.logical_and(is_direct, jnp.logical_not(is_home)))
    def _():
        for k in ALONG:
            greet(line_id(HOME, k))

    @pl.when(is_home)
    def _():
        for k, dy in cross:
            if k != 0:
                greet(cross_id(k, dy))

        @pl.loop(1, NZ)
        def _(zz):
            greet(z_id(zz))

        @pl.loop(1, DIRECT)
        def _(zz):
            for k in ALONG:
                greet(line_id(zz, k))

    loads[4].wait()
    rate_t = poles_in[0]
    weight_t = poles_in[1] * jnp.sqrt(2.0 * rate_t)
    odd = lax.broadcasted_iota(jnp.int32, (SUB, ROWS), 0) % 2 == 1
    for m in range(MODES):
        rate = jnp.where(odd, rate_t[m : m + 1, ROWS:], rate_t[m : m + 1, :ROWS])
        d_tab[m] = jnp.exp(-rate)
        block_decay_tab[m] = jnp.exp(-rate * ROWS)
        plane_decay_tab[m] = jnp.exp(-rate * (ROWS * NX))
        w_tab[m] = jnp.where(odd, weight_t[m : m + 1, ROWS:], weight_t[m : m + 1, :ROWS])

    loads[0].wait()
    loads[1].wait()
    for j in range(SUB):
        rows = pl.ds(j * ROWS, ROWS)
        product = k_in[rows, :].astype(F32) * v_in[rows, :].astype(F32)
        x_kv[pl.ds(j, ROWS, stride=SUB), :] = product.T
    loads[2].wait()
    loads[3].wait()
    for j in range(SUB):
        rows = pl.ds(j * ROWS, ROWS)
        product = g_in[rows, :].astype(F32) * q_in[rows, :].astype(F32)
        x_g[pl.ds(j, ROWS, stride=SUB), :] = product.T

    def at(t):
        return pl.ds(pl.multiple_of(t * SUB, SUB), SUB)

    zero = jnp.zeros((SUB, ROWS), F32)
    for p in range(PLANE):
        a_send[p, 4] = zero
    for first in range(0, MODES, GROUP):
        modes = range(first, first + GROUP)
        d = [d_tab[m] for m in modes]

        def end_step(t, carry, d=d):
            ahead, back, acc = carry
            here, there = at(t), at(ROWS - 1 - t)
            value, grad, late = x_kv[here, :], x_g[here, :], x_g[there, :]
            ahead = tuple(d[i] * ahead[i] + value for i in range(GROUP))
            back = tuple(d[i] * back[i] + late for i in range(GROUP))
            acc = tuple(acc[i] + grad * ahead[i] for i in range(GROUP))
            return ahead, back, acc

        start = ((zero,) * GROUP,) * 3
        ahead, back, acc = lax.fori_loop(0, ROWS, end_step, start, unroll=16)
        for i, m in enumerate(modes):
            a_send[m // 2, m % 2] = ahead[i]
            a_send[m // 2, 2 + m % 2] = back[i]
            rows = 2 * (m % 2)
            a_send[m // 2, 4, rows : rows + 2, :] = tree_sum(
                acc[i][2 * r : 2 * r + 2, :] for r in range(4)
            )

    at_home = (NCH - 1) * NY + NZ - 1 + (DIRECT - 1) * len(ALONG)
    beyond = jnp.where(is_home, at_home, jnp.where(is_direct, NX, 1))
    pl.semaphore_wait(barrier, len(plane) + beyond)

    def remote(src, dst, send_sem, recv_sem, device):
        return pltpu.make_async_remote_copy(
            src_ref=src, dst_ref=dst, send_sem=send_sem, recv_sem=recv_sem,
            device_id=device, device_id_type=MESH,
        )

    a_copies = [
        remote(a_send.at[p], a_recv.at[a], a_send_sem.at[i], a_recv_sem.at[i], device)
        for i, (p, device) in enumerate(zip(plane, plane_ids))
    ]
    for copy in a_copies:
        copy.start()
    a_recv[a] = a_send[a]

    for first in range(0, MODES, GROUP):
        modes = range(first, first + GROUP)
        d = [d_tab[m] for m in modes]
        w = [w_tab[m] for m in modes]

        def local_step(t, carry, d=d, w=w, first=first):
            ahead, back = carry
            here, there = at(t), at(ROWS - 1 - t)
            value, late = x_kv[here, :], x_g[there, :]
            ahead = tuple(d[i] * ahead[i] + value for i in range(GROUP))
            back = tuple(d[i] * back[i] + late for i in range(GROUP))
            out = tree_sum(w[i] * ahead[i] for i in range(GROUP))
            out_grad = tree_sum(w[i] * back[i] for i in range(GROUP))
            if first:
                out = out + c_out[here, :]
                out_grad = out_grad + c_grad[there, :]
            c_out[here, :] = out
            c_grad[there, :] = out_grad
            return ahead, back

        lax.fori_loop(0, ROWS, local_step, ((zero,) * GROUP,) * 2, unroll=16)

    mine = pl.ds(2 * a, 2)
    d2, block_decay, plane_decay = d_tab[mine], block_decay_tab[mine], plane_decay_tab[mine]
    for copy in a_copies:
        copy.wait_recv()

    def over_repeats(value):
        rows_tmp[...] = value
        return [tree_sum(rows_tmp[i, 2 * r : 2 * r + 2, :] for r in range(4)) for i in range(2)]

    between = jnp.zeros((2, SUB, ROWS), F32)
    for yy in range(NY):
        run = jnp.zeros((2, SUB, ROWS), F32)
        for xx in range(NX):
            slot = yy * NX + xx
            between = between + d2 * a_recv[slot, 2:4] * run
            run = block_decay * run + a_recv[slot, 0:2]
        b_send[2 * yy : 2 * yy + 2] = run
        run = jnp.zeros((2, SUB, ROWS), F32)
        for xx in reversed(range(NX)):
            run = block_decay * run + a_recv[yy * NX + xx, 2:4]
        b_send[4 + 2 * yy : 6 + 2 * yy] = run
    b_send[8] = tree_sum(a_recv[slot, 4] for slot in range(PLANE))
    for i, rows in enumerate(over_repeats(between)):
        b_send[8, 2 * i : 2 * i + 2, :] = b_send[8, 2 * i : 2 * i + 2, :] + rows

    def to_home(zz):
        return remote(b_send, b_recv.at[zz], b_send_sem, b_recv_sem.at[zz], z_id(HOME))

    def answer(zz):
        return remote(owner_out.at[zz], c_recv, c_send_sem.at[zz], c_recv_sem, z_id(zz))

    def result(k, dy):
        return remote(
            r_send, r_recv.at[ch, y], r_send_sem.at[k, dy], r_recv_sem.at[k, dy], cross_id(k, dy)
        )

    def summed(zz):
        return remote(r_sum, r_sum, g_send_sem.at[zz], g_recv_sem, z_id(zz))

    def along(zz, k):
        return remote(
            r_sum, f_recv.at[x], f_send_sem.at[zz, k], f_recv_sem.at[k], line_id(zz, k)
        )

    def pass_on():
        for k in ALONG:
            along(z, k).start()
        f_recv[x] = r_sum[...]

    @pl.when(jnp.logical_not(is_home))
    def _():
        to_home(z).start()

    @pl.when(is_home)
    def _():
        b_recv[HOME] = b_send[...]
        for zz in range(NZ):
            if zz != HOME:
                to_home(zz).wait_recv()
        run = jnp.zeros((2, SUB, ROWS), F32)
        between = jnp.zeros((2, SUB, ROWS), F32)
        for yy in range(NY):
            for zz in range(NZ):
                owner_out[zz, 2 * yy : 2 * yy + 2] = run
                between = between + d2 * b_recv[zz, 4 + 2 * yy : 6 + 2 * yy] * run
                run = plane_decay * run + b_recv[zz, 2 * yy : 2 * yy + 2]
        within = tree_sum(b_recv[zz, 8] for zz in range(NZ))
        for i, rows in enumerate(over_repeats(between)):
            r_send[i] = rows + within[2 * i : 2 * i + 2, :]
        for k, dy in cross:
            result(k, dy).start()
        run = jnp.zeros((2, SUB, ROWS), F32)
        for yy in reversed(range(NY)):
            for zz in reversed(range(NZ)):
                owner_out[zz, 4 + 2 * yy : 6 + 2 * yy] = run
                run = plane_decay * run + b_recv[zz, 4 + 2 * yy : 6 + 2 * yy]
        for zz in ANSWER_FIRST:
            answer(zz).start()
        r_recv[ch, y] = r_send[...]
        c_recv[...] = owner_out[HOME]

    @pl.when(jnp.logical_not(is_home))
    def _():
        answer(z).wait_recv()

    for yy in range(NY):
        run = c_recv[2 * yy : 2 * yy + 2]
        for xx in range(NX):
            slot = yy * NX + xx
            e_send[slot, 0:2] = run
            run = block_decay * run + a_recv[slot, 0:2]
        run = c_recv[4 + 2 * yy : 6 + 2 * yy]
        for xx in reversed(range(NX)):
            slot = yy * NX + xx
            e_send[slot, 2:4] = run
            run = block_decay * run + a_recv[slot, 2:4]
    e_copies = [
        remote(e_send.at[p], e_recv.at[a], e_send_sem.at[i], e_recv_sem.at[i], device)
        for i, (p, device) in enumerate(zip(plane, plane_ids))
    ]
    for copy in e_copies:
        copy.start()
    e_recv[a] = e_send[a]

    @pl.when(is_home)
    def _():
        for zz in ANSWER_LATER:
            answer(zz).start()

    @pl.when(is_home)
    def _():
        for k, dy in cross:
            result(k, dy).wait_recv()
        r_sum[...] = (r_recv[0] + r_recv[1]) + (r_recv[2] + r_recv[3])
        for zz in RESULT_ORDER:
            if zz == HOME:
                pass_on()
            elif zz < DIRECT:
                for k in ALONG + (0,):
                    along(zz, k).start()
            else:
                summed(zz).start()

    @pl.when(jnp.logical_not(is_direct))
    def _():
        summed(z).wait_recv()
        pass_on()

    for copy in e_copies:
        copy.wait_recv()
    d = [d_tab[m] for m in range(MODES)]
    w = [w_tab[m] for m in range(MODES)]
    ahead = tuple(w[m] * e_recv[m // 2, m % 2] for m in range(MODES))
    back = tuple(w[m] * e_recv[m // 2, 2 + m % 2] for m in range(MODES))

    def carry_step(t, carry):
        ahead, back = carry
        here, there = at(t), at(ROWS - 1 - t)
        ahead = tuple(d[n] * ahead[n] for n in range(len(d)))
        back = tuple(d[n] * back[n] for n in range(len(d)))
        c_out[here, :] = c_out[here, :] + tree_sum(ahead)
        c_grad[there, :] = c_grad[there, :] + tree_sum(back)
        return ahead, back

    lax.fori_loop(0, ROWS, carry_step, (ahead, back), unroll=16)

    for j in range(SUB):
        rows = pl.ds(j * ROWS, ROWS)
        lanes = pl.ds(j, ROWS, stride=SUB)
        gq_out[rows, :] = (g_in[rows, :].astype(F32) * c_out[lanes, :].T).astype(jnp.bfloat16)
        conv_grad = c_grad[lanes, :].T
        gk_out[rows, :] = (conv_grad * v_in[rows, :].astype(F32)).astype(jnp.bfloat16)
        gv_out[rows, :] = (conv_grad * k_in[rows, :].astype(F32)).astype(jnp.bfloat16)

    for k in ALONG:
        along(z, k).wait_recv()
    pl.when(jnp.logical_and(is_direct, jnp.logical_not(is_home)))(along(z, 0).wait_recv)
    for m in range(MODES):
        for half in range(2):
            cols = slice(half * ROWS, (half + 1) * ROWS)
            res_out[m : m + 1, cols] = f_recv[m // 2 % NX, m // 2 // NX, m % 2, half : half + 1, :]
    res_out[...] = res_out[...] * (jnp.sqrt(2.0 * poles_in[0]) * norm)
    for copy in a_copies + e_copies:
        copy.wait_send()
    @pl.when(jnp.logical_not(is_home))
    def _():
        to_home(z).wait_send()

    @pl.when(is_home)
    def _():
        @pl.loop(1, NZ)
        def _(zz):
            answer(zz).wait_send()

        for k, dy in cross:
            result(k, dy).wait_send()

        @pl.loop(1, DIRECT)
        def _(zz):
            for k in range(NX):
                along(zz, k).wait_send()

        @pl.loop(DIRECT, NZ)
        def _(zz):
            summed(zz).wait_send()

    @pl.when(jnp.logical_or(is_home, jnp.logical_not(is_direct)))
    def _():
        for k in ALONG:
            along(z, k).wait_send()


def scan_call(norm, q, k, v, g, poles):
    hbm = pl.BlockSpec(memory_space=pltpu.HBM)
    big = pltpu.VMEM((CHN, ROWS), F32)
    half = pltpu.VMEM((CHN, ROWS), jnp.bfloat16)
    table = pltpu.VMEM((MODES, SUB, ROWS), F32)
    dma = pltpu.SemaphoreType.DMA
    wide = jax.ShapeDtypeStruct((CHN, ROWS), jnp.bfloat16)
    return pl.pallas_call(
        functools.partial(scan_kernel, norm),
        out_shape=(wide, wide, wide, jax.ShapeDtypeStruct((MODES, FG), F32)),
        in_specs=[hbm] * 5,
        out_specs=(pl.BlockSpec(memory_space=pltpu.VMEM),) * 4,
        scratch_shapes=[
            half, half, half, half, pltpu.VMEM((2, MODES, FG), F32),
            big, big, big, big,
            table, table, table, table,
            pltpu.VMEM((PLANE, 5, SUB, ROWS), F32),
            pltpu.VMEM((PLANE, 5, SUB, ROWS), F32),
            pltpu.VMEM((2, SUB, ROWS), F32),
            pltpu.VMEM((9, SUB, ROWS), F32),
            pltpu.VMEM((NZ, 9, SUB, ROWS), F32),
            pltpu.VMEM((NZ, 8, SUB, ROWS), F32),
            pltpu.VMEM((8, SUB, ROWS), F32),
            pltpu.VMEM((2, 2, ROWS), F32),
            pltpu.VMEM((NCH, NY, 2, 2, ROWS), F32),
            pltpu.VMEM((NY, 2, 2, ROWS), F32),
            pltpu.VMEM((PLANE, 4, SUB, ROWS), F32),
            pltpu.VMEM((PLANE, 4, SUB, ROWS), F32),
            pltpu.VMEM((NX, NY, 2, 2, ROWS), F32),
            dma((5,)),
            dma((PLANE - 1,)), dma((PLANE - 1,)), dma, dma((NZ,)), dma((NZ,)), dma,
            dma((NCH, NY)), dma((NCH, NY)), dma((NZ,)), dma,
            dma((PLANE - 1,)), dma((PLANE - 1,)), dma((NZ, NX)), dma((NX,)),
        ],
        compiler_params=pltpu.CompilerParams(
            collective_id=0, has_side_effects=True, vmem_limit_bytes=54336 * 2**10
        ),
        name="scan_states",
    )(q, k, v, g, poles)


def finish_kernel(*refs):
    half = len(refs) // 2
    srcs, dsts, sems = refs[:half], refs[half : 2 * half], refs[2 * half]
    copies = [pltpu.make_async_copy(srcs[i], dsts[i], sems.at[i]) for i in range(half)]
    for copy in copies:
        copy.start()
    for copy in copies:
        copy.wait()


def finish_call(*results):
    n = len(results)
    anywhere = pl.BlockSpec(memory_space=pl.ANY)
    return pl.pallas_call(
        finish_kernel,
        out_shape=tuple(jax.ShapeDtypeStruct(r.shape, r.dtype) for r in results),
        in_specs=[anywhere] * n,
        out_specs=(anywhere,) * n,
        scratch_shapes=[pltpu.SemaphoreType.DMA((n,))],
        compiler_params=pltpu.CompilerParams(vmem_limit_bytes=4 * 2**20),
        name="finish",
    )(*results)


def local(q_branch, k_branch, v_branch, grad_gated, decay_rates, residue):
    norm = 1.0 / math.sqrt(q_branch.shape[1] * lax.axis_size("ctx"))
    poles = jnp.stack([decay_rates.T, residue.T])
    grad_q, grad_k, grad_v, res = finish_call(
        *scan_call(norm, q_branch, k_branch, v_branch, grad_gated, poles)
    )
    return grad_q, grad_k, grad_v, res.T


def solution(mesh):
    in_specs = (P("ch", "ctx"), P("ch", "ctx"), P("ch", "ctx"), P("ch", "ctx"), P(), P())
    out_specs = (P("ch", "ctx"), P("ch", "ctx"), P("ch", "ctx"), P())
    return jax.shard_map(local, mesh=mesh, in_specs=in_specs, out_specs=out_specs, check_vma=False)
```

```python
import functools
import math

import jax
import jax.numpy as jnp
from jax import lax
from jax.experimental import pallas as pl
from jax.experimental.pallas import tpu as pltpu
from jax.sharding import PartitionSpec as P

MESH = pl.DeviceIdType.MESH
F32 = jnp.float32

NX, NZ, NY, NCH = 4, 16, 2, 4
PLANE = NX * NY
MODES = 16
FG = 256
CHN = 1024
ROWS = 128
SUB = 8
GROUP = 8
HOME = 0
ANSWER_FIRST = (1, 2, 3, 4, 5, 6, 7, 8)
ANSWER_LATER = (9, 15, 10, 14, 11, 13, 12)
DIRECT = 5
RESULT_ORDER = (1, 2, 5, 6, 7, 8, 0, 3, 4, 9, 10, 11, 12, 13, 14, 15)
ALONG = (2, 1, 3)
NEAR = ((0, 1), (0, 3), (1, 0))
FAR = ((1, 2), (1, 1), (1, 3), (0, 2))


def tree_sum(terms):
    terms = list(terms)
    while len(terms) > 1:
        terms = [
            terms[i] + terms[i + 1] if i + 1 < len(terms) else terms[i]
            for i in range(0, len(terms), 2)
        ]
    return terms[0]


def scan_kernel(
    norm,
    q_hbm, k_hbm, v_hbm, g_hbm, poles_hbm,
    gq_out, gk_out, gv_out, res_out,
    q_in, k_in, v_in, g_in, poles_in,
    x_kv, x_g, c_out, c_grad,
    d_tab, w_tab, plane_decay_tab, block_decay_tab,
    a_send, a_recv, rows_tmp, b_send, b_recv, owner_out, c_recv, r_send, r_recv, r_sum, e_send, e_recv,
    f_recv, in_sem,
    a_send_sem, a_recv_sem, b_send_sem, b_recv_sem, c_send_sem, c_recv_sem,
    r_send_sem, r_recv_sem, g_send_sem, g_recv_sem, e_send_sem, e_recv_sem, f_send_sem, f_recv_sem,
):
    ctx, ch = lax.axis_index("ctx"), lax.axis_index("ch")
    y, z, x = lax.div(ctx, NX * NZ), lax.rem(lax.div(ctx, NX), NZ), lax.rem(ctx, NX)
    a = y * NX + x
    is_home = z == HOME
    is_direct = z < DIRECT
    x_plus = [lax.rem(x + k, NX) for k in range(NX)]
    y_plus = [lax.rem(y + k, NY) for k in range(NY)]
    ch_plus = [lax.rem(ch + k, NCH) for k in range(NCH)]
    column = y * (NZ * NX) + x

    plane = [y_plus[dy] * NX + x_plus[dx] for dy, dx in FAR + NEAR]
    plane_ids = [((y_plus[dy] * NZ + z) * NX + x_plus[dx], ch) for dy, dx in FAR + NEAR]

    def line_id(zz, k):
        return (y * NZ + zz) * NX + x_plus[k], ch

    def z_id(zz):
        return column + zz * NX, ch

    def cross_id(k, dy):
        return (y_plus[dy] * NZ + HOME) * NX + x, ch_plus[k]

    cross = [(k, dy) for k in range(NCH) for dy in reversed(range(NY)) if k or dy]

    loads = [
        pltpu.make_async_copy(src, dst, in_sem.at[i])
        for i, (src, dst) in enumerate(
            [
                (k_hbm, k_in), (v_hbm, v_in), (g_hbm, g_in), (q_hbm, q_in),
                (poles_hbm, poles_in),
            ]
        )
    ]
    for i in (4, 0, 1, 2, 3):
        loads[i].start()

    barrier = pltpu.get_barrier_semaphore()

    def greet(device):
        pl.semaphore_signal(barrier, inc=1, device_id=device, device_id_type=MESH)

    for device in plane_ids:
        greet(device)

    @pl.when(jnp.logical_not(is_home))
    def _():
        greet(z_id(HOME))

    @pl.when(jnp.logical_and(is_direct, jnp.logical_not(is_home)))
    def _():
        for k in ALONG:
            greet(line_id(HOME, k))

    @pl.when(is_home)
    def _():
        for k, dy in cross:
            if k != 0:
                greet(cross_id(k, dy))

        @pl.loop(1, NZ)
        def _(zz):
            greet(z_id(zz))

        @pl.loop(1, DIRECT)
        def _(zz):
            for k in ALONG:
                greet(line_id(zz, k))

    loads[4].wait()
    rate_t = poles_in[0]
    weight_t = poles_in[1] * jnp.sqrt(2.0 * rate_t)
    odd = lax.broadcasted_iota(jnp.int32, (SUB, ROWS), 0) % 2 == 1
    for m in range(MODES):
        rate = jnp.where(odd, rate_t[m : m + 1, ROWS:], rate_t[m : m + 1, :ROWS])
        d_tab[m] = jnp.exp(-rate)
        block_decay_tab[m] = jnp.exp(-rate * ROWS)
        plane_decay_tab[m] = jnp.exp(-rate * (ROWS * NX))
        w_tab[m] = jnp.where(odd, weight_t[m : m + 1, ROWS:], weight_t[m : m + 1, :ROWS])

    loads[0].wait()
    loads[1].wait()
    for j in range(SUB):
        rows = pl.ds(j * ROWS, ROWS)
        product = k_in[rows, :].astype(F32) * v_in[rows, :].astype(F32)
        x_kv[pl.ds(j, ROWS, stride=SUB), :] = product.T
    loads[2].wait()
    loads[3].wait()
    for j in range(SUB):
        rows = pl.ds(j * ROWS, ROWS)
        product = g_in[rows, :].astype(F32) * q_in[rows, :].astype(F32)
        x_g[pl.ds(j, ROWS, stride=SUB), :] = product.T

    def at(t):
        return pl.ds(pl.multiple_of(t * SUB, SUB), SUB)

    zero = jnp.zeros((SUB, ROWS), F32)
    for p in range(PLANE):
        a_send[p, 4] = zero
    for first in range(0, MODES, GROUP):
        modes = range(first, first + GROUP)
        d = [d_tab[m] for m in modes]

        def end_step(t, carry, d=d):
            ahead, back, acc = carry
            here, there = at(t), at(ROWS - 1 - t)
            value, grad, late = x_kv[here, :], x_g[here, :], x_g[there, :]
            ahead = tuple(d[i] * ahead[i] + value for i in range(GROUP))
            back = tuple(d[i] * back[i] + late for i in range(GROUP))
            acc = tuple(acc[i] + grad * ahead[i] for i in range(GROUP))
            return ahead, back, acc

        start = ((zero,) * GROUP,) * 3
        ahead, back, acc = lax.fori_loop(0, ROWS, end_step, start, unroll=16)
        for i, m in enumerate(modes):
            a_send[m // 2, m % 2] = ahead[i]
            a_send[m // 2, 2 + m % 2] = back[i]
            rows = 2 * (m % 2)
            a_send[m // 2, 4, rows : rows + 2, :] = tree_sum(
                acc[i][2 * r : 2 * r + 2, :] for r in range(4)
            )

    at_home = (NCH - 1) * NY + NZ - 1 + (DIRECT - 1) * len(ALONG)
    beyond = jnp.where(is_home, at_home, jnp.where(is_direct, NX, 1))
    pl.semaphore_wait(barrier, len(plane) + beyond)

    def remote(src, dst, send_sem, recv_sem, device):
        return pltpu.make_async_remote_copy(
            src_ref=src, dst_ref=dst, send_sem=send_sem, recv_sem=recv_sem,
            device_id=device, device_id_type=MESH,
        )

    a_copies = [
        remote(a_send.at[p], a_recv.at[a], a_send_sem.at[i], a_recv_sem.at[i], device)
        for i, (p, device) in enumerate(zip(plane, plane_ids))
    ]
    for copy in a_copies:
        copy.start()
    a_recv[a] = a_send[a]

    for first in range(0, MODES, GROUP):
        modes = range(first, first + GROUP)
        d = [d_tab[m] for m in modes]
        w = [w_tab[m] for m in modes]

        def local_step(t, carry, d=d, w=w, first=first):
            ahead, back = carry
            here, there = at(t), at(ROWS - 1 - t)
            value, late = x_kv[here, :], x_g[there, :]
            ahead = tuple(d[i] * ahead[i] + value for i in range(GROUP))
            back = tuple(d[i] * back[i] + late for i in range(GROUP))
            out = tree_sum(w[i] * ahead[i] for i in range(GROUP))
            out_grad = tree_sum(w[i] * back[i] for i in range(GROUP))
            if first:
                out = out + c_out[here, :]
                out_grad = out_grad + c_grad[there, :]
            c_out[here, :] = out
            c_grad[there, :] = out_grad
            return ahead, back

        lax.fori_loop(0, ROWS, local_step, ((zero,) * GROUP,) * 2, unroll=16)

    mine = pl.ds(2 * a, 2)
    d2, block_decay, plane_decay = d_tab[mine], block_decay_tab[mine], plane_decay_tab[mine]
    for copy in a_copies:
        copy.wait_recv()

    def over_repeats(value):
        rows_tmp[...] = value
        return [tree_sum(rows_tmp[i, 2 * r : 2 * r + 2, :] for r in range(4)) for i in range(2)]

    between = jnp.zeros((2, SUB, ROWS), F32)
    for yy in range(NY):
        run = jnp.zeros((2, SUB, ROWS), F32)
        for xx in range(NX):
            slot = yy * NX + xx
            between = between + d2 * a_recv[slot, 2:4] * run
            run = block_decay * run + a_recv[slot, 0:2]
        b_send[2 * yy : 2 * yy + 2] = run
        run = jnp.zeros((2, SUB, ROWS), F32)
        for xx in reversed(range(NX)):
            run = block_decay * run + a_recv[yy * NX + xx, 2:4]
        b_send[4 + 2 * yy : 6 + 2 * yy] = run
    b_send[8] = tree_sum(a_recv[slot, 4] for slot in range(PLANE))
    for i, rows in enumerate(over_repeats(between)):
        b_send[8, 2 * i : 2 * i + 2, :] = b_send[8, 2 * i : 2 * i + 2, :] + rows

    def to_home(zz):
        return remote(b_send, b_recv.at[zz], b_send_sem, b_recv_sem.at[zz], z_id(HOME))

    def answer(zz):
        return remote(owner_out.at[zz], c_recv, c_send_sem.at[zz], c_recv_sem, z_id(zz))

    def result(k, dy):
        return remote(
            r_send, r_recv.at[ch, y], r_send_sem.at[k, dy], r_recv_sem.at[k, dy], cross_id(k, dy)
        )

    def summed(zz):
        return remote(r_sum, r_sum, g_send_sem.at[zz], g_recv_sem, z_id(zz))

    def along(zz, k):
        return remote(
            r_sum, f_recv.at[x], f_send_sem.at[zz, k], f_recv_sem.at[k], line_id(zz, k)
        )

    def pass_on():
        for k in ALONG:
            along(z, k).start()
        f_recv[x] = r_sum[...]

    @pl.when(jnp.logical_not(is_home))
    def _():
        to_home(z).start()

    @pl.when(is_home)
    def _():
        b_recv[HOME] = b_send[...]
        for zz in range(NZ):
            if zz != HOME:
                to_home(zz).wait_recv()
        run = jnp.zeros((2, SUB, ROWS), F32)
        between = jnp.zeros((2, SUB, ROWS), F32)
        for yy in range(NY):
            for zz in range(NZ):
                owner_out[zz, 2 * yy : 2 * yy + 2] = run
                between = between + d2 * b_recv[zz, 4 + 2 * yy : 6 + 2 * yy] * run
                run = plane_decay * run + b_recv[zz, 2 * yy : 2 * yy + 2]
        within = tree_sum(b_recv[zz, 8] for zz in range(NZ))
        for i, rows in enumerate(over_repeats(between)):
            r_send[i] = rows + within[2 * i : 2 * i + 2, :]
        for k, dy in cross:
            result(k, dy).start()
        run = jnp.zeros((2, SUB, ROWS), F32)
        for yy in reversed(range(NY)):
            for zz in reversed(range(NZ)):
                owner_out[zz, 4 + 2 * yy : 6 + 2 * yy] = run
                run = plane_decay * run + b_recv[zz, 4 + 2 * yy : 6 + 2 * yy]
        for zz in ANSWER_FIRST:
            answer(zz).start()
        r_recv[ch, y] = r_send[...]
        c_recv[...] = owner_out[HOME]

    @pl.when(jnp.logical_not(is_home))
    def _():
        answer(z).wait_recv()

    for yy in range(NY):
        run = c_recv[2 * yy : 2 * yy + 2]
        for xx in range(NX):
            slot = yy * NX + xx
            e_send[slot, 0:2] = run
            run = block_decay * run + a_recv[slot, 0:2]
        run = c_recv[4 + 2 * yy : 6 + 2 * yy]
        for xx in reversed(range(NX)):
            slot = yy * NX + xx
            e_send[slot, 2:4] = run
            run = block_decay * run + a_recv[slot, 2:4]
    e_copies = [
        remote(e_send.at[p], e_recv.at[a], e_send_sem.at[i], e_recv_sem.at[i], device)
        for i, (p, device) in enumerate(zip(plane, plane_ids))
    ]
    for copy in e_copies:
        copy.start()
    e_recv[a] = e_send[a]

    @pl.when(is_home)
    def _():
        for zz in ANSWER_LATER:
            answer(zz).start()

    @pl.when(is_home)
    def _():
        for k, dy in cross:
            result(k, dy).wait_recv()
        r_sum[...] = (r_recv[0] + r_recv[1]) + (r_recv[2] + r_recv[3])
        for zz in RESULT_ORDER:
            if zz == HOME:
                pass_on()
            elif zz < DIRECT:
                for k in ALONG + (0,):
                    along(zz, k).start()
            else:
                summed(zz).start()

    @pl.when(jnp.logical_not(is_direct))
    def _():
        summed(z).wait_recv()
        pass_on()

    for copy in e_copies:
        copy.wait_recv()
    d = [d_tab[m] for m in range(MODES)]
    w = [w_tab[m] for m in range(MODES)]
    ahead = tuple(w[m] * e_recv[m // 2, m % 2] for m in range(MODES))
    back = tuple(w[m] * e_recv[m // 2, 2 + m % 2] for m in range(MODES))

    def carry_step(t, carry):
        ahead, back = carry
        here, there = at(t), at(ROWS - 1 - t)
        ahead = tuple(d[n] * ahead[n] for n in range(len(d)))
        back = tuple(d[n] * back[n] for n in range(len(d)))
        c_out[here, :] = c_out[here, :] + tree_sum(ahead)
        c_grad[there, :] = c_grad[there, :] + tree_sum(back)
        return ahead, back

    lax.fori_loop(0, ROWS, carry_step, (ahead, back), unroll=16)

    for j in range(SUB):
        rows = pl.ds(j * ROWS, ROWS)
        lanes = pl.ds(j, ROWS, stride=SUB)
        gq_out[rows, :] = (g_in[rows, :].astype(F32) * c_out[lanes, :].T).astype(jnp.bfloat16)
        conv_grad = c_grad[lanes, :].T
        gk_out[rows, :] = (conv_grad * v_in[rows, :].astype(F32)).astype(jnp.bfloat16)
        gv_out[rows, :] = (conv_grad * k_in[rows, :].astype(F32)).astype(jnp.bfloat16)

    for k in ALONG:
        along(z, k).wait_recv()
    pl.when(jnp.logical_and(is_direct, jnp.logical_not(is_home)))(along(z, 0).wait_recv)
    for m in range(MODES):
        for half in range(2):
            cols = slice(half * ROWS, (half + 1) * ROWS)
            res_out[m : m + 1, cols] = f_recv[m // 2 % NX, m // 2 // NX, m % 2, half : half + 1, :]
    res_out[...] = res_out[...] * (jnp.sqrt(2.0 * poles_in[0]) * norm)
    for copy in a_copies + e_copies:
        copy.wait_send()
    @pl.when(jnp.logical_not(is_home))
    def _():
        to_home(z).wait_send()

    @pl.when(is_home)
    def _():
        @pl.loop(1, NZ)
        def _(zz):
            answer(zz).wait_send()

        for k, dy in cross:
            result(k, dy).wait_send()

        @pl.loop(1, DIRECT)
        def _(zz):
            for k in range(NX):
                along(zz, k).wait_send()

        @pl.loop(DIRECT, NZ)
        def _(zz):
            summed(zz).wait_send()

    @pl.when(jnp.logical_or(is_home, jnp.logical_not(is_direct)))
    def _():
        for k in ALONG:
            along(z, k).wait_send()


def scan_call(norm, q, k, v, g, poles):
    hbm = pl.BlockSpec(memory_space=pltpu.HBM)
    big = pltpu.VMEM((CHN + SUB, ROWS), F32)
    half = pltpu.VMEM((CHN, ROWS), jnp.bfloat16)
    table = pltpu.VMEM((MODES, SUB, ROWS), F32)
    dma = pltpu.SemaphoreType.DMA
    wide = jax.ShapeDtypeStruct((CHN, ROWS), jnp.bfloat16)
    return pl.pallas_call(
        functools.partial(scan_kernel, norm),
        out_shape=(wide, wide, wide, jax.ShapeDtypeStruct((MODES, FG), F32)),
        in_specs=[hbm] * 5,
        out_specs=(pl.BlockSpec(memory_space=pltpu.VMEM),) * 4,
        scratch_shapes=[
            half, half, half, half, pltpu.VMEM((2, MODES, FG), F32),
            big, big, big, big,
            table, table, table, table,
            pltpu.VMEM((PLANE, 5, SUB, ROWS), F32),
            pltpu.VMEM((PLANE, 5, SUB, ROWS), F32),
            pltpu.VMEM((2, SUB, ROWS), F32),
            pltpu.VMEM((9, SUB, ROWS), F32),
            pltpu.VMEM((NZ, 9, SUB, ROWS), F32),
            pltpu.VMEM((NZ, 8, SUB, ROWS), F32),
            pltpu.VMEM((8, SUB, ROWS), F32),
            pltpu.VMEM((2, 2, ROWS), F32),
            pltpu.VMEM((NCH, NY, 2, 2, ROWS), F32),
            pltpu.VMEM((NY, 2, 2, ROWS), F32),
            pltpu.VMEM((PLANE, 4, SUB, ROWS), F32),
            pltpu.VMEM((PLANE, 4, SUB, ROWS), F32),
            pltpu.VMEM((NX, NY, 2, 2, ROWS), F32),
            dma((5,)),
            dma((PLANE - 1,)), dma((PLANE - 1,)), dma, dma((NZ,)), dma((NZ,)), dma,
            dma((NCH, NY)), dma((NCH, NY)), dma((NZ,)), dma,
            dma((PLANE - 1,)), dma((PLANE - 1,)), dma((NZ, NX)), dma((NX,)),
        ],
        compiler_params=pltpu.CompilerParams(
            collective_id=0, has_side_effects=True, vmem_limit_bytes=54336 * 2**10
        ),
        name="scan_states",
    )(q, k, v, g, poles)


def finish_kernel(*refs):
    half = len(refs) // 2
    srcs, dsts, sems = refs[:half], refs[half : 2 * half], refs[2 * half]
    copies = [pltpu.make_async_copy(srcs[i], dsts[i], sems.at[i]) for i in range(half)]
    for copy in copies:
        copy.start()
    for copy in copies:
        copy.wait()


def finish_call(*results):
    n = len(results)
    anywhere = pl.BlockSpec(memory_space=pl.ANY)
    return pl.pallas_call(
        finish_kernel,
        out_shape=tuple(jax.ShapeDtypeStruct(r.shape, r.dtype) for r in results),
        in_specs=[anywhere] * n,
        out_specs=(anywhere,) * n,
        scratch_shapes=[pltpu.SemaphoreType.DMA((n,))],
        compiler_params=pltpu.CompilerParams(vmem_limit_bytes=4 * 2**20),
        name="finish",
    )(*results)


def local(q_branch, k_branch, v_branch, grad_gated, decay_rates, residue):
    norm = 1.0 / math.sqrt(q_branch.shape[1] * lax.axis_size("ctx"))
    poles = jnp.stack([decay_rates.T, residue.T])
    grad_q, grad_k, grad_v, res = finish_call(
        *scan_call(norm, q_branch, k_branch, v_branch, grad_gated, poles)
    )
    return grad_q, grad_k, grad_v, res.T


def solution(mesh):
    in_specs = (P("ch", "ctx"), P("ch", "ctx"), P("ch", "ctx"), P("ch", "ctx"), P(), P())
    out_specs = (P("ch", "ctx"), P("ch", "ctx"), P("ch", "ctx"), P())
    return jax.shard_map(local, mesh=mesh, in_specs=in_specs, out_specs=out_specs, check_vma=False)
```

```python
import functools
import math

import jax
import jax.numpy as jnp
from jax import lax
from jax.experimental import pallas as pl
from jax.experimental.pallas import tpu as pltpu
from jax.sharding import PartitionSpec as P

MESH = pl.DeviceIdType.MESH
F32 = jnp.float32

NX, NZ, NY, NCH = 4, 16, 2, 4
PLANE = NX * NY
MODES = 16
FG = 256
CHN = 1024
ROWS = 128
SUB = 8
GROUP = 8
HOME = 0
ANSWER_FIRST = (1, 2, 3, 4, 5, 6, 7, 8)
ANSWER_LATER = (9, 15, 10, 14, 11, 13, 12)
DIRECT = 5
RESULT_ORDER = (1, 2, 5, 6, 7, 8, 0, 3, 4, 9, 10, 11, 12, 13, 14, 15)
ALONG = (2, 1, 3)
NEAR = ((0, 1), (0, 3), (1, 0))
FAR = ((1, 2), (1, 1), (1, 3), (0, 2))


def tree_sum(terms):
    terms = list(terms)
    while len(terms) > 1:
        terms = [
            terms[i] + terms[i + 1] if i + 1 < len(terms) else terms[i]
            for i in range(0, len(terms), 2)
        ]
    return terms[0]


def scan_kernel(
    norm,
    q_hbm, k_hbm, v_hbm, g_hbm, poles_hbm,
    gq_out, gk_out, gv_out, res_out,
    q_in, k_in, v_in, g_in, poles_in,
    x_kv, x_g, c_out, c_grad,
    d_tab, w_tab, plane_decay_tab, block_decay_tab,
    a_send, a_recv, rows_tmp, b_send, b_recv, owner_out, c_recv, r_send, r_recv, r_sum, e_send, e_recv,
    f_recv, in_sem,
    a_send_sem, a_recv_sem, b_send_sem, b_recv_sem, c_send_sem, c_recv_sem,
    r_send_sem, r_recv_sem, g_send_sem, g_recv_sem, e_send_sem, e_recv_sem, f_send_sem, f_recv_sem,
):
    ctx, ch = lax.axis_index("ctx"), lax.axis_index("ch")
    y, z, x = lax.div(ctx, NX * NZ), lax.rem(lax.div(ctx, NX), NZ), lax.rem(ctx, NX)
    a = y * NX + x
    is_home = z == HOME
    is_direct = z < DIRECT
    x_plus = [lax.rem(x + k, NX) for k in range(NX)]
    y_plus = [lax.rem(y + k, NY) for k in range(NY)]
    ch_plus = [lax.rem(ch + k, NCH) for k in range(NCH)]
    column = y * (NZ * NX) + x

    plane = [y_plus[dy] * NX + x_plus[dx] for dy, dx in FAR + NEAR]
    plane_ids = [((y_plus[dy] * NZ + z) * NX + x_plus[dx], ch) for dy, dx in FAR + NEAR]

    def line_id(zz, k):
        return (y * NZ + zz) * NX + x_plus[k], ch

    def z_id(zz):
        return column + zz * NX, ch

    def cross_id(k, dy):
        return (y_plus[dy] * NZ + HOME) * NX + x, ch_plus[k]

    cross = [(k, dy) for k in (2, 1, 3, 0) for dy in reversed(range(NY)) if k or dy]

    loads = [
        pltpu.make_async_copy(src, dst, in_sem.at[i])
        for i, (src, dst) in enumerate(
            [
                (k_hbm, k_in), (v_hbm, v_in), (g_hbm, g_in), (q_hbm, q_in),
                (poles_hbm, poles_in),
            ]
        )
    ]
    for i in (4, 0, 1, 2, 3):
        loads[i].start()

    barrier = pltpu.get_barrier_semaphore()

    def greet(device):
        pl.semaphore_signal(barrier, inc=1, device_id=device, device_id_type=MESH)

    for device in plane_ids:
        greet(device)

    @pl.when(jnp.logical_not(is_home))
    def _():
        greet(z_id(HOME))

    @pl.when(jnp.logical_and(is_direct, jnp.logical_not(is_home)))
    def _():
        for k in ALONG:
            greet(line_id(HOME, k))

    @pl.when(is_home)
    def _():
        for k, dy in cross:
            if k != 0:
                greet(cross_id(k, dy))

        @pl.loop(1, NZ)
        def _(zz):
            greet(z_id(zz))

        @pl.loop(1, DIRECT)
        def _(zz):
            for k in ALONG:
                greet(line_id(zz, k))

    loads[4].wait()
    rate_t = poles_in[0]
    weight_t = poles_in[1] * jnp.sqrt(2.0 * rate_t)
    odd = lax.broadcasted_iota(jnp.int32, (SUB, ROWS), 0) % 2 == 1
    for m in range(MODES):
        rate = jnp.where(odd, rate_t[m : m + 1, ROWS:], rate_t[m : m + 1, :ROWS])
        d_tab[m] = jnp.exp(-rate)
        block_decay_tab[m] = jnp.exp(-rate * ROWS)
        plane_decay_tab[m] = jnp.exp(-rate * (ROWS * NX))
        w_tab[m] = jnp.where(odd, weight_t[m : m + 1, ROWS:], weight_t[m : m + 1, :ROWS])

    loads[0].wait()
    loads[1].wait()
    for j in range(SUB):
        rows = pl.ds(j * ROWS, ROWS)
        product = k_in[rows, :].astype(F32) * v_in[rows, :].astype(F32)
        x_kv[pl.ds(j, ROWS, stride=SUB), :] = product.T
    loads[2].wait()
    loads[3].wait()
    for j in range(SUB):
        rows = pl.ds(j * ROWS, ROWS)
        product = g_in[rows, :].astype(F32) * q_in[rows, :].astype(F32)
        x_g[pl.ds(j, ROWS, stride=SUB), :] = product.T

    def at(t):
        return pl.ds(pl.multiple_of(t * SUB, SUB), SUB)

    zero = jnp.zeros((SUB, ROWS), F32)
    for p in range(PLANE):
        a_send[p, 4] = zero
    for first in range(0, MODES, GROUP):
        modes = range(first, first + GROUP)
        d = [d_tab[m] for m in modes]

        def end_step(t, carry, d=d):
            ahead, back, acc = carry
            here, there = at(t), at(ROWS - 1 - t)
            value, grad, late = x_kv[here, :], x_g[here, :], x_g[there, :]
            ahead = tuple(d[i] * ahead[i] + value for i in range(GROUP))
            back = tuple(d[i] * back[i] + late for i in range(GROUP))
            acc = tuple(acc[i] + grad * ahead[i] for i in range(GROUP))
            return ahead, back, acc

        start = ((zero,) * GROUP,) * 3
        ahead, back, acc = lax.fori_loop(0, ROWS, end_step, start, unroll=16)
        for i, m in enumerate(modes):
            a_send[m // 2, m % 2] = ahead[i]
            a_send[m // 2, 2 + m % 2] = back[i]
            rows = 2 * (m % 2)
            a_send[m // 2, 4, rows : rows + 2, :] = tree_sum(
                acc[i][2 * r : 2 * r + 2, :] for r in range(4)
            )

    at_home = (NCH - 1) * NY + NZ - 1 + (DIRECT - 1) * len(ALONG)
    beyond = jnp.where(is_home, at_home, jnp.where(is_direct, NX, 1))
    pl.semaphore_wait(barrier, len(plane) + beyond)

    def remote(src, dst, send_sem, recv_sem, device):
        return pltpu.make_async_remote_copy(
            src_ref=src, dst_ref=dst, send_sem=send_sem, recv_sem=recv_sem,
            device_id=device, device_id_type=MESH,
        )

    a_copies = [
        remote(a_send.at[p], a_recv.at[a], a_send_sem.at[i], a_recv_sem.at[i], device)
        for i, (p, device) in enumerate(zip(plane, plane_ids))
    ]
    for copy in a_copies:
        copy.start()
    a_recv[a] = a_send[a]

    for first in range(0, MODES, GROUP):
        modes = range(first, first + GROUP)
        d = [d_tab[m] for m in modes]
        w = [w_tab[m] for m in modes]

        def local_step(t, carry, d=d, w=w, first=first):
            ahead, back = carry
            here, there = at(t), at(ROWS - 1 - t)
            value, late = x_kv[here, :], x_g[there, :]
            ahead = tuple(d[i] * ahead[i] + value for i in range(GROUP))
            back = tuple(d[i] * back[i] + late for i in range(GROUP))
            out = tree_sum(w[i] * ahead[i] for i in range(GROUP))
            out_grad = tree_sum(w[i] * back[i] for i in range(GROUP))
            if first:
                out = out + c_out[here, :]
                out_grad = out_grad + c_grad[there, :]
            c_out[here, :] = out
            c_grad[there, :] = out_grad
            return ahead, back

        lax.fori_loop(0, ROWS, local_step, ((zero,) * GROUP,) * 2, unroll=16)

    mine = pl.ds(2 * a, 2)
    d2, block_decay, plane_decay = d_tab[mine], block_decay_tab[mine], plane_decay_tab[mine]
    for copy in a_copies:
        copy.wait_recv()

    def over_repeats(value):
        rows_tmp[...] = value
        return [tree_sum(rows_tmp[i, 2 * r : 2 * r + 2, :] for r in range(4)) for i in range(2)]

    between = jnp.zeros((2, SUB, ROWS), F32)
    for yy in range(NY):
        run = jnp.zeros((2, SUB, ROWS), F32)
        for xx in range(NX):
            slot = yy * NX + xx
            between = between + d2 * a_recv[slot, 2:4] * run
            run = block_decay * run + a_recv[slot, 0:2]
        b_send[2 * yy : 2 * yy + 2] = run
        run = jnp.zeros((2, SUB, ROWS), F32)
        for xx in reversed(range(NX)):
            run = block_decay * run + a_recv[yy * NX + xx, 2:4]
        b_send[4 + 2 * yy : 6 + 2 * yy] = run
    b_send[8] = tree_sum(a_recv[slot, 4] for slot in range(PLANE))
    for i, rows in enumerate(over_repeats(between)):
        b_send[8, 2 * i : 2 * i + 2, :] = b_send[8, 2 * i : 2 * i + 2, :] + rows

    def to_home(zz):
        return remote(b_send, b_recv.at[zz], b_send_sem, b_recv_sem.at[zz], z_id(HOME))

    def answer(zz):
        return remote(owner_out.at[zz], c_recv, c_send_sem.at[zz], c_recv_sem, z_id(zz))

    def result(k, dy):
        return remote(
            r_send, r_recv.at[ch, y], r_send_sem.at[k, dy], r_recv_sem.at[k, dy], cross_id(k, dy)
        )

    def summed(zz):
        return remote(r_sum, r_sum, g_send_sem.at[zz], g_recv_sem, z_id(zz))

    def along(zz, k):
        return remote(
            r_sum, f_recv.at[x], f_send_sem.at[zz, k], f_recv_sem.at[k], line_id(zz, k)
        )

    def pass_on():
        for k in ALONG:
            along(z, k).start()
        f_recv[x] = r_sum[...]

    @pl.when(jnp.logical_not(is_home))
    def _():
        to_home(z).start()

    @pl.when(is_home)
    def _():
        b_recv[HOME] = b_send[...]
        for zz in range(NZ):
            if zz != HOME:
                to_home(zz).wait_recv()
        run = jnp.zeros((2, SUB, ROWS), F32)
        between = jnp.zeros((2, SUB, ROWS), F32)
        for yy in range(NY):
            for zz in range(NZ):
                owner_out[zz, 2 * yy : 2 * yy + 2] = run
                between = between + d2 * b_recv[zz, 4 + 2 * yy : 6 + 2 * yy] * run
                run = plane_decay * run + b_recv[zz, 2 * yy : 2 * yy + 2]
        within = tree_sum(b_recv[zz, 8] for zz in range(NZ))
        for i, rows in enumerate(over_repeats(between)):
            r_send[i] = rows + within[2 * i : 2 * i + 2, :]
        for k, dy in cross:
            result(k, dy).start()
        run = jnp.zeros((2, SUB, ROWS), F32)
        for yy in reversed(range(NY)):
            for zz in reversed(range(NZ)):
                owner_out[zz, 4 + 2 * yy : 6 + 2 * yy] = run
                run = plane_decay * run + b_recv[zz, 4 + 2 * yy : 6 + 2 * yy]
        for zz in ANSWER_FIRST:
            answer(zz).start()
        r_recv[ch, y] = r_send[...]
        c_recv[...] = owner_out[HOME]

    @pl.when(jnp.logical_not(is_home))
    def _():
        answer(z).wait_recv()

    for yy in range(NY):
        run = c_recv[2 * yy : 2 * yy + 2]
        for xx in range(NX):
            slot = yy * NX + xx
            e_send[slot, 0:2] = run
            run = block_decay * run + a_recv[slot, 0:2]
        run = c_recv[4 + 2 * yy : 6 + 2 * yy]
        for xx in reversed(range(NX)):
            slot = yy * NX + xx
            e_send[slot, 2:4] = run
            run = block_decay * run + a_recv[slot, 2:4]
    e_copies = [
        remote(e_send.at[p], e_recv.at[a], e_send_sem.at[i], e_recv_sem.at[i], device)
        for i, (p, device) in enumerate(zip(plane, plane_ids))
    ]
    for copy in e_copies:
        copy.start()
    e_recv[a] = e_send[a]

    @pl.when(is_home)
    def _():
        for zz in ANSWER_LATER:
            answer(zz).start()

    @pl.when(is_home)
    def _():
        for k, dy in cross:
            result(k, dy).wait_recv()
        r_sum[...] = (r_recv[0] + r_recv[1]) + (r_recv[2] + r_recv[3])
        for zz in RESULT_ORDER:
            if zz == HOME:
                pass_on()
            elif zz < DIRECT:
                for k in ALONG + (0,):
                    along(zz, k).start()
            else:
                summed(zz).start()

    @pl.when(jnp.logical_not(is_direct))
    def _():
        summed(z).wait_recv()
        pass_on()

    for copy in e_copies:
        copy.wait_recv()
    d = [d_tab[m] for m in range(MODES)]
    w = [w_tab[m] for m in range(MODES)]
    ahead = tuple(w[m] * e_recv[m // 2, m % 2] for m in range(MODES))
    back = tuple(w[m] * e_recv[m // 2, 2 + m % 2] for m in range(MODES))

    def carry_step(t, carry):
        ahead, back = carry
        here, there = at(t), at(ROWS - 1 - t)
        ahead = tuple(d[n] * ahead[n] for n in range(len(d)))
        back = tuple(d[n] * back[n] for n in range(len(d)))
        c_out[here, :] = c_out[here, :] + tree_sum(ahead)
        c_grad[there, :] = c_grad[there, :] + tree_sum(back)
        return ahead, back

    lax.fori_loop(0, ROWS, carry_step, (ahead, back), unroll=16)

    for j in range(SUB):
        rows = pl.ds(j * ROWS, ROWS)
        lanes = pl.ds(j, ROWS, stride=SUB)
        gq_out[rows, :] = (g_in[rows, :].astype(F32) * c_out[lanes, :].T).astype(jnp.bfloat16)
        conv_grad = c_grad[lanes, :].T
        gk_out[rows, :] = (conv_grad * v_in[rows, :].astype(F32)).astype(jnp.bfloat16)
        gv_out[rows, :] = (conv_grad * k_in[rows, :].astype(F32)).astype(jnp.bfloat16)

    for k in ALONG:
        along(z, k).wait_recv()
    pl.when(jnp.logical_and(is_direct, jnp.logical_not(is_home)))(along(z, 0).wait_recv)
    for m in range(MODES):
        for half in range(2):
            cols = slice(half * ROWS, (half + 1) * ROWS)
            res_out[m : m + 1, cols] = f_recv[m // 2 % NX, m // 2 // NX, m % 2, half : half + 1, :]
    res_out[...] = res_out[...] * (jnp.sqrt(2.0 * poles_in[0]) * norm)
    for copy in a_copies + e_copies:
        copy.wait_send()
    @pl.when(jnp.logical_not(is_home))
    def _():
        to_home(z).wait_send()

    @pl.when(is_home)
    def _():
        @pl.loop(1, NZ)
        def _(zz):
            answer(zz).wait_send()

        for k, dy in cross:
            result(k, dy).wait_send()

        @pl.loop(1, DIRECT)
        def _(zz):
            for k in range(NX):
                along(zz, k).wait_send()

        @pl.loop(DIRECT, NZ)
        def _(zz):
            summed(zz).wait_send()

    @pl.when(jnp.logical_or(is_home, jnp.logical_not(is_direct)))
    def _():
        for k in ALONG:
            along(z, k).wait_send()


def scan_call(norm, q, k, v, g, poles):
    hbm = pl.BlockSpec(memory_space=pltpu.HBM)
    big = pltpu.VMEM((CHN + SUB, ROWS), F32)
    half = pltpu.VMEM((CHN, ROWS), jnp.bfloat16)
    table = pltpu.VMEM((MODES, SUB, ROWS), F32)
    dma = pltpu.SemaphoreType.DMA
    wide = jax.ShapeDtypeStruct((CHN, ROWS), jnp.bfloat16)
    return pl.pallas_call(
        functools.partial(scan_kernel, norm),
        out_shape=(wide, wide, wide, jax.ShapeDtypeStruct((MODES, FG), F32)),
        in_specs=[hbm] * 5,
        out_specs=(pl.BlockSpec(memory_space=pltpu.VMEM),) * 4,
        scratch_shapes=[
            half, half, half, half, pltpu.VMEM((2, MODES, FG), F32),
            big, big, big, big,
            table, table, table, table,
            pltpu.VMEM((PLANE, 5, SUB, ROWS), F32),
            pltpu.VMEM((PLANE, 5, SUB, ROWS), F32),
            pltpu.VMEM((2, SUB, ROWS), F32),
            pltpu.VMEM((9, SUB, ROWS), F32),
            pltpu.VMEM((NZ, 9, SUB, ROWS), F32),
            pltpu.VMEM((NZ, 8, SUB, ROWS), F32),
            pltpu.VMEM((8, SUB, ROWS), F32),
            pltpu.VMEM((2, 2, ROWS), F32),
            pltpu.VMEM((NCH, NY, 2, 2, ROWS), F32),
            pltpu.VMEM((NY, 2, 2, ROWS), F32),
            pltpu.VMEM((PLANE, 4, SUB, ROWS), F32),
            pltpu.VMEM((PLANE, 4, SUB, ROWS), F32),
            pltpu.VMEM((NX, NY, 2, 2, ROWS), F32),
            dma((5,)),
            dma((PLANE - 1,)), dma((PLANE - 1,)), dma, dma((NZ,)), dma((NZ,)), dma,
            dma((NCH, NY)), dma((NCH, NY)), dma((NZ,)), dma,
            dma((PLANE - 1,)), dma((PLANE - 1,)), dma((NZ, NX)), dma((NX,)),
        ],
        compiler_params=pltpu.CompilerParams(
            collective_id=0, has_side_effects=True, vmem_limit_bytes=54336 * 2**10
        ),
        name="scan_states",
    )(q, k, v, g, poles)


def finish_kernel(*refs):
    half = len(refs) // 2
    srcs, dsts, sems = refs[:half], refs[half : 2 * half], refs[2 * half]
    copies = [pltpu.make_async_copy(srcs[i], dsts[i], sems.at[i]) for i in range(half)]
    for copy in copies:
        copy.start()
    for copy in copies:
        copy.wait()


def finish_call(*results):
    n = len(results)
    anywhere = pl.BlockSpec(memory_space=pl.ANY)
    return pl.pallas_call(
        finish_kernel,
        out_shape=tuple(jax.ShapeDtypeStruct(r.shape, r.dtype) for r in results),
        in_specs=[anywhere] * n,
        out_specs=(anywhere,) * n,
        scratch_shapes=[pltpu.SemaphoreType.DMA((n,))],
        compiler_params=pltpu.CompilerParams(vmem_limit_bytes=4 * 2**20),
        name="finish",
    )(*results)


def local(q_branch, k_branch, v_branch, grad_gated, decay_rates, residue):
    norm = 1.0 / math.sqrt(q_branch.shape[1] * lax.axis_size("ctx"))
    poles = jnp.stack([decay_rates.T, residue.T])
    grad_q, grad_k, grad_v, res = finish_call(
        *scan_call(norm, q_branch, k_branch, v_branch, grad_gated, poles)
    )
    return grad_q, grad_k, grad_v, res.T


def solution(mesh):
    in_specs = (P("ch", "ctx"), P("ch", "ctx"), P("ch", "ctx"), P("ch", "ctx"), P(), P())
    out_specs = (P("ch", "ctx"), P("ch", "ctx"), P("ch", "ctx"), P())
    return jax.shard_map(local, mesh=mesh, in_specs=in_specs, out_specs=out_specs, check_vma=False)
```
